256 devices in a mesh: gx: 4 (over x), gy: 8 (over y, core), gz: 8 (over z).
Axes of the slice: x: 4, y: 4, z: 8, core: 2. Of those that a mesh axis runs over, the one named last changes fastest.
Arguments:
- points: float32 [4, 8, 8, 3, 512], P('gx', 'gy', 'gz'), may hold values from -0.5 to 0.5, as said below
- band_index: int32 [4, 8, 8, 6, 64], P('gx', 'gy', 'gz'), may hold values from 0 to 512, as said below
- source: float32 [4, 8, 8, 512], P('gx', 'gy', 'gz'), may hold values from -8 to 8
- fine_first: float32 [4, 8, 8, 4, 64], P('gx', 'gy', 'gz'), may hold values from -4 to 4
- fine_mid: float32 [4, 8, 8, 2, 64, 64], P('gx', 'gy', 'gz'), may hold values from -0.75 to 0.75
- fine_last: float32 [4, 8, 8, 3, 64], P('gx', 'gy', 'gz'), may hold values from -1.5 to 1.5
- column_first: float32 [4, 8, 4, 64], P('gx', 'gy'), may hold values from -4 to 4
- column_mid: float32 [4, 8, 2, 64, 64], P('gx', 'gy'), may hold values from -0.75 to 0.75
- column_last: float32 [4, 8, 3, 64], P('gx', 'gy'), may hold values from -1.5 to 1.5
- global_first: float32 [4, 64], replicated, may hold values from -4 to 4
- global_mid: float32 [2, 64, 64], replicated, may hold values from -0.75 to 0.75
- global_last: float32 [3, 64], replicated, may hold values from -1.5 to 1.5
Outputs:
- residual: float32 [4, 8, 8, 512], P('gx', 'gy', 'gz')
- fine_first_grad: float32 [4, 8, 8, 4, 64], P('gx', 'gy', 'gz')
- fine_mid_grad: float32 [4, 8, 8, 2, 64, 64], P('gx', 'gy', 'gz')
- fine_last_grad: float32 [4, 8, 8, 3, 64], P('gx', 'gy', 'gz')
- column_first_grad: float32 [4, 8, 4, 64], P('gx', 'gy')
- column_mid_grad: float32 [4, 8, 2, 64, 64], P('gx', 'gy')
- column_last_grad: float32 [4, 8, 3, 64], P('gx', 'gy')
- global_first_grad: float32 [4, 64], replicated
- global_mid_grad: float32 [2, 64, 64], replicated
- global_last_grad: float32 [3, 64], replicated
- loss: float32 [], replicated
The draws below stay inside these ranges and needn't reach their ends.
Inputs may be any that keep to these rules, and one draw needn't show every extreme that they name: Each point lies inside its cell. A point is within 1/8 of at most one face of its cell, and exactly the points named in band_index are within 1/8 of a face. `band_index`: row f of a subdomain lists distinct points within 1/8 of face f (faces: lower and upper along x, then y, then z), then padding entries equal to 512. The lists of one subdomain are disjoint. Each list holds 32 to 64 points, and in every subdomain some list is full.
All inputs are finite; a program needn't handle non-finite values.
Results may differ from the reference program's by a relative error of at most 0.0003.
Values sent between devices are 32-bit elements; how exact they have to be, the bound alone decides.
A program may use at most 128 MiB of HBM per device.

```python
import jax
import jax.numpy as jnp
from jax import lax

W = 64
MIDS = 2
P_DEV = 512
BAND = 64
NGX = 4
NGY = 8
NGZ = 8


band_depth = 0.125


def band_layout(key):
    leading = (NGX, NGY, NGZ)
    key_count, key_full, key_order = jax.random.split(key, 3)
    counts = jax.random.randint(key_count, leading + (6,), BAND // 2, BAND + 1)
    full_face = jax.random.randint(key_full, leading, 0, 6)
    counts = jnp.where(jnp.arange(6)[None, None, None, :] == full_face[..., None], BAND, counts)
    scores = jax.random.randint(key_order, leading + (P_DEV,), 0, 1 << 17) * P_DEV + jnp.arange(P_DEV)
    order = jnp.argsort(scores, axis=-1, stable=True).astype(jnp.int32)
    slots = order[..., :6 * BAND].reshape(leading + (6, BAND))
    band = jnp.where(jnp.arange(BAND)[None, None, None, None, :] < counts[..., None], slots, P_DEV)
    ranks = jnp.argsort(order, axis=-1, stable=True).astype(jnp.int32)
    face_slot = ranks // BAND
    within = ranks % BAND
    count_at = jnp.take_along_axis(counts, jnp.clip(face_slot, 0, 5), axis=-1)
    face_of = jnp.where((face_slot < 6) & (within < count_at), face_slot, -1)
    return (band.astype(jnp.int32), face_of)


def draw_band_index(key, part):
    band, face_of = band_layout(key)
    return band


def draw_points(key, part):
    band, face_of = band_layout(key)
    key = jax.random.fold_in(key, 11)
    key_inner, key_depth = jax.random.split(key)
    leading = (NGX, NGY, NGZ)
    inner = (jax.random.uniform(key_inner, leading + (3, P_DEV), jnp.float32) - 0.5) * (1.0 - 2.0 * band_depth)
    depth = jax.random.uniform(key_depth, leading + (P_DEV,), jnp.float32)
    rows = [inner[..., direction, :] for direction in range(3)]
    for face_id in range(6):
        direction = face_id // 2
        facing = float(2 * (face_id % 2) - 1)
        rows[direction] = jnp.where(face_of == face_id, facing * (0.5 - band_depth * depth), rows[direction])
    return jnp.stack(rows, axis=-2).astype(jnp.float32)


def block_levels(key, dims, pieces, smallest, largest):
    factor_of, own = 1.0, jax.random.fold_in(key, 6)
    for dim, parts in pieces:
        heights = jnp.exp(jax.random.uniform(jax.random.fold_in(own, dim), (parts,), jnp.float32, smallest / len(pieces), largest / len(pieces)))
        factor_of = factor_of * jnp.repeat(heights, dims[dim] // parts).reshape([-1 if axis == dim else 1 for axis in range(len(dims))])
    return factor_of


def gaussian(stream_key, shape, width, reach, cuts=(), held_as=jnp.bfloat16):
    entries = jax.random.normal(stream_key, shape, jnp.float32) * width
    if len(cuts) > 0:
        entries = block_levels(stream_key, shape, cuts, -0.22, 0.18) * entries
    return jnp.clip(entries, min=-reach, max=reach).astype(held_as)


def setup_inputs(seed: int = 0) -> dict:
    arg_keys = jax.random.split(jax.random.key(seed), 13)
    points = draw_points(jax.random.fold_in(arg_keys[12], 71), 0)
    band_index = draw_band_index(jax.random.fold_in(arg_keys[12], 71), 0)
    source = gaussian(arg_keys[2], (NGX, NGY, NGZ, P_DEV), 2.0, 8.0, ((0, 4), (1, 8), (2, 8)), jnp.float32)
    fine_first = gaussian(arg_keys[3], (NGX, NGY, NGZ, 4, W), 1.0, 4.0, ((0, 4), (1, 8), (2, 8)), jnp.float32)
    fine_mid = gaussian(arg_keys[4], (NGX, NGY, NGZ, MIDS, W, W), W ** -0.5, 0.75, ((0, 4), (1, 8), (2, 8)), jnp.float32)
    fine_last = gaussian(arg_keys[5], (NGX, NGY, NGZ, MIDS + 1, W), 0.3, 1.5, ((0, 4), (1, 8), (2, 8)), jnp.float32)
    column_first = gaussian(arg_keys[6], (NGX, NGY, 4, W), 1.0, 4.0, ((0, 4), (1, 8)), jnp.float32)
    column_mid = gaussian(arg_keys[7], (NGX, NGY, MIDS, W, W), W ** -0.5, 0.75, ((0, 4), (1, 8)), jnp.float32)
    column_last = gaussian(arg_keys[8], (NGX, NGY, MIDS + 1, W), 0.3, 1.5, ((0, 4), (1, 8)), jnp.float32)
    global_first = gaussian(arg_keys[9], (4, W), 1.0, 4.0, (), jnp.float32)
    global_mid = gaussian(arg_keys[10], (MIDS, W, W), W ** -0.5, 0.75, (), jnp.float32)
    global_last = gaussian(arg_keys[11], (MIDS + 1, W), 0.3, 1.5, (), jnp.float32)
    return dict(points=points, band_index=band_index, source=source, fine_first=fine_first, fine_mid=fine_mid, fine_last=fine_last, column_first=column_first, column_mid=column_mid, column_last=column_last, global_first=global_first, global_mid=global_mid, global_last=global_last)


band_depth = 0.125
wave_square = 4.0
highest = lax.Precision.HIGHEST

def network_terms(first_layer, mid_layers, last_rows, location, factor):
    tangent_in = first_layer[:3] * factor[:, None]
    preact = jnp.einsum('dw,dn->wn', first_layer[:3], location, precision=highest) + first_layer[3][:, None]
    hidden = jnp.tanh(preact)
    sloped = 1.0 - hidden * hidden
    tangent = sloped[None] * tangent_in[:, :, None]
    second = -2.0 * hidden[None] * tangent * tangent_in[:, :, None]
    for layer in range(mid_layers.shape[0]):
        stacked = jnp.concatenate([hidden[None], tangent, second], 0)
        mapped = jnp.einsum('ow,swn->son', mid_layers[layer], stacked, precision=highest)
        preact = mapped[0] + last_rows[layer][:, None]
        first_dir = mapped[1:4]
        hidden = jnp.tanh(preact)
        sloped = 1.0 - hidden * hidden
        tangent = sloped[None] * first_dir
        second = sloped[None] * mapped[4:7] - 2.0 * hidden[None] * tangent * first_dir
    net_value = jnp.einsum('w,wn->n', last_rows[-1], hidden, precision=highest)
    net_grad = jnp.einsum('w,dwn->dn', last_rows[-1], tangent, precision=highest)
    net_laplace = jnp.einsum('w,dwn->n', last_rows[-1], second, precision=highest)
    return (net_value, net_grad, net_laplace)

def window_terms(along, facing):
    depth = jnp.minimum((0.5 - facing * along) / band_depth, 1.0)
    smooth = (15.0 * depth - 10.0 * depth ** 3 + 3.0 * depth ** 5) / 8.0
    rising = 15.0 * (1.0 - depth * depth) ** 2 / 8.0
    curving = -7.5 * depth * (1.0 - depth * depth)
    blend = 0.5 * (1.0 - smooth)
    slope = 0.5 * facing * rising / band_depth
    bend = -0.5 * curving / (band_depth * band_depth)
    return (blend, slope, bend)

def device_residual(location, band, source, own_net, near_nets, column_net, global_net, position, extent):
    count = location.shape[1]
    two_scale = jnp.full((3,), 2.0, jnp.float32)
    net_value, net_grad, net_laplace = network_terms(*own_net, 2.0 * location, two_scale)
    own_weight = jnp.ones_like(net_value)
    own_slope = [jnp.zeros_like(net_value) for direction in range(3)]
    own_curve = jnp.zeros_like(net_value)
    near_value = jnp.zeros_like(net_value)
    near_laplace = jnp.zeros_like(net_value)
    for face_id in range(6):
        direction = face_id // 2
        facing = 2 * (face_id % 2) - 1
        beyond = position[direction] + facing
        present = ((beyond >= 0) & (beyond < extent[direction])).astype(jnp.float32)
        blend, slope, bend = window_terms(location[direction], float(facing))
        blend = blend * present
        slope = slope * present
        bend = bend * present
        own_weight = own_weight - blend
        own_slope[direction] = own_slope[direction] - slope
        own_curve = own_curve - bend
        members = band[face_id]
        clipped = jnp.minimum(members, count - 1)
        shifted = location[:, clipped].at[direction].add(-float(facing))
        far_value, far_grad, far_laplace = network_terms(*near_nets[face_id], 2.0 * shifted, two_scale)
        near_blend = blend[clipped]
        near_slope = slope[clipped]
        near_bend = bend[clipped]
        near_value = near_value.at[members].add(near_blend * far_value, mode='drop')
        near_laplace = near_laplace.at[members].add(near_blend * far_laplace + 2.0 * near_slope * far_grad[direction] + near_bend * far_value, mode='drop')
    fine_value = own_weight * net_value + near_value
    fine_laplace = own_weight * net_laplace + 2.0 * (own_slope[0] * net_grad[0] + own_slope[1] * net_grad[1] + own_slope[2] * net_grad[2]) + own_curve * net_value + near_laplace
    place = [position[direction].astype(jnp.float32) for direction in range(3)]
    column_in = jnp.stack([2.0 * location[0], 2.0 * location[1], (2.0 * place[2] + 1.0 + 2.0 * location[2]) / extent[2] - 1.0])
    column_scale = jnp.asarray([2.0, 2.0, 2.0 / extent[2]], jnp.float32)
    column_value, column_grad, column_laplace = network_terms(*column_net, column_in, column_scale)
    global_in = jnp.stack([(2.0 * place[direction] + 1.0 + 2.0 * location[direction]) / extent[direction] - 1.0 for direction in range(3)])
    global_scale = jnp.asarray([2.0 / extent[0], 2.0 / extent[1], 2.0 / extent[2]], jnp.float32)
    global_value, global_grad, global_laplace = network_terms(*global_net, global_in, global_scale)
    return fine_laplace + column_laplace + global_laplace + wave_square * (fine_value + column_value + global_value) - source

def reference(points, band_index, source, fine_first, fine_mid, fine_last, column_first, column_mid, column_last, global_first, global_mid, global_last):
    extent = (NGX, NGY, NGZ)

    def residual_all(fine_nets, column_nets, global_net):
        padded = tuple((jnp.pad(array, ((1, 1), (1, 1), (1, 1)) + ((0, 0),) * (array.ndim - 3)) for array in fine_nets))

        def per_device(flat_index):
            cell_x = flat_index // (NGY * NGZ)
            cell_y = flat_index // NGZ % NGY
            cell_z = flat_index % NGZ
            own_net = tuple((array[cell_x + 1, cell_y + 1, cell_z + 1] for array in padded))
            near_nets = []
            for face_id in range(6):
                direction = face_id // 2
                facing = 2 * (face_id % 2) - 1
                offset = [1, 1, 1]
                offset[direction] = 1 + facing
                near_nets.append(tuple((array[cell_x + offset[0], cell_y + offset[1], cell_z + offset[2]] for array in padded)))
            column_net = tuple((array[cell_x, cell_y] for array in column_nets))
            return device_residual(points[cell_x, cell_y, cell_z], band_index[cell_x, cell_y, cell_z], source[cell_x, cell_y, cell_z], own_net, near_nets, column_net, global_net, (cell_x, cell_y, cell_z), extent)
        flat_all = lax.map(jax.checkpoint(per_device), jnp.arange(NGX * NGY * NGZ, dtype=jnp.int32))
        return flat_all.reshape(NGX, NGY, NGZ, P_DEV)
    residual, pullback = jax.vjp(residual_all, (fine_first, fine_mid, fine_last), (column_first, column_mid, column_last), (global_first, global_mid, global_last))
    fine_grads, column_grads, global_grads = pullback(residual / P_DEV)
    loss = jnp.sum(residual * residual) / (2.0 * P_DEV)
    return (residual, fine_grads[0], fine_grads[1], fine_grads[2], column_grads[0], column_grads[1], column_grads[2], global_grads[0], global_grads[1], global_grads[2], loss)
```

```python
import functools

import jax
import jax.numpy as jnp
from jax import lax
from jax.experimental import pallas as pl
from jax.experimental.pallas import tpu as pltpu
from jax.sharding import PartitionSpec as P

MESH = pl.DeviceIdType.MESH
AXES = ("gx", "gy", "gz")
f32, bf16 = jnp.float32, jnp.bfloat16
wave_square = 4.0
inverse_depth = 8.0
NT = (((1,), (1,)), ((), ()))


def split(value):
    high = value.astype(bf16)
    return high, (value - high.astype(f32)).astype(bf16)


def three(value):
    first = value.astype(bf16)
    rest = value - first.astype(f32)
    second = rest.astype(bf16)
    return first, second, (rest - second.astype(f32)).astype(bf16)


def left(matrix):
    high = matrix.astype(bf16).astype(f32)
    return jnp.concatenate([high, high, matrix - high], 1).astype(bf16)


def right(high, low):
    return jnp.concatenate([high, low, high], 0)


def dot(a, b):
    return jnp.dot(a, b, preferred_element_type=f32)


def dot_nt(a, b):
    return lax.dot_general(a, b, NT, preferred_element_type=f32)


def window(depth, facing):
    square = depth * depth
    smooth = depth * (15.0 - 10.0 * square + 3.0 * square * square) / 8.0
    blend = 0.5 * (1.0 - smooth)
    slope = (0.5 * inverse_depth * 15.0 / 8.0) * facing * (1.0 - square) * (1.0 - square)
    bend = (0.5 * inverse_depth * inverse_depth * 7.5) * depth * (1.0 - square)
    return blend, slope, bend


def kernel(
    sizes,
    chunk,
    points,
    band,
    source,
    fine_first,
    fine_mid,
    fine_last,
    column_first,
    column_mid,
    column_last,
    global_first,
    global_mid,
    global_last,
    residual_out,
    fine_first_out,
    fine_mid_out,
    fine_last_out,
    column_first_out,
    column_mid_out,
    column_last_out,
    global_first_out,
    global_mid_out,
    global_last_out,
    loss_out,
    nets,
    grads,
    f1,
    f2,
    b2,
    b1h,
    b1s,
    b1p,
    cols,
    xp,
    xpb,
    alpha,
    x0,
    x1,
    h0s,
    a1,
    a2,
    res,
    xf,
    xfb,
    falpha,
    fx0,
    fx1,
    fh0s,
    fa1,
    fa2,
    fdelta,
    hot,
    back,
    gchunks,
    cchunks,
    grs,
    gys,
    gxs,
    gag,
    crs,
    cag,
    halo_send,
    halo_recv,
    back_send,
    back_recv,
    grs_send,
    grs_recv,
    gy_send,
    gy_recv,
    gx_send,
    gx_recv,
    gag_send,
    gag_recv,
    crs_send,
    crs_recv,
    cag_send,
    cag_recv,
):
    me = tuple(lax.axis_index(axis) for axis in AXES)
    count = points.shape[1]
    slots = band.shape[1]
    pair = 2 * slots

    def peer(axis, offset):
        other = list(me)
        other[axis] = lax.rem(me[axis] + (offset + sizes[axis]), sizes[axis])
        return tuple(other)

    barrier = pltpu.get_barrier_semaphore()
    greeted = 0
    for axis in range(3):
        for offset in range(1, sizes[axis]):
            pl.semaphore_signal(barrier, inc=1, device_id=peer(axis, offset), device_id_type=MESH)
            greeted += 1

    def pack(net, first, mid, last):
        nets[net, 0:64, :] = jnp.concatenate([mid[0], mid[1]], 1)
        nets[net, 64:68, 0:64] = first[...]
        nets[net, 68:71, 0:64] = last[...]
        nets[net, 71:72, 0:64] = jnp.zeros((1, 64), f32)
        nets[net, 64:72, 64:128] = jnp.zeros((8, 64), f32)

    pack(2, fine_first, fine_mid, fine_last)
    pl.semaphore_wait(barrier, greeted)

    def halo(face):
        axis, up = face // 2, face % 2
        return pltpu.make_async_remote_copy(
            src_ref=nets.at[2],
            dst_ref=nets.at[3 + (face ^ 1)],
            send_sem=halo_send.at[face],
            recv_sem=halo_recv.at[face ^ 1],
            device_id=peer(axis, 2 * up - 1),
            device_id_type=MESH,
        )

    for face in range(6):
        halo(face).start()

    pack(1, column_first, column_mid, column_last)
    pack(0, global_first, global_mid, global_last)

    place = [me[axis].astype(f32) for axis in range(3)]

    def affine(net):
        if isinstance(net, int) and net >= 3:
            face = net - 3
            shift = [0.0, 0.0, 0.0]
            shift[face // 2] = -2.0 * (2 * (face % 2) - 1)
            return [2.0, 2.0, 2.0], shift
        scale, shift = [], []
        for axis in range(3):
            fitted_scale = 2.0 / sizes[axis]
            fitted_shift = (2.0 * place[axis] + 1.0) * (1.0 / sizes[axis]) - 1.0
            fitted = (net == 0) if axis < 2 else (net <= 1)
            scale.append(jnp.where(fitted, fitted_scale, 2.0))
            shift.append(jnp.where(fitted, fitted_shift, 0.0))
        return scale, shift

    def prepare(net, scale, shift):
        mats = nets[net, 0:64, :]
        turned = mats.T
        rows = nets[net, 64:72, :]
        turned_rows = rows.T
        m1 = mats[:, 0:64]
        m1t = turned[0:64]
        row = [scale[d] * rows[d : d + 1, 0:64] for d in range(3)]
        col = [scale[d] * turned_rows[0:64, d : d + 1] for d in range(3)]
        square_row = -2.0 * (row[0] * row[0] + row[1] * row[1] + row[2] * row[2])
        square_col = -2.0 * (col[0] * col[0] + col[1] * col[1] + col[2] * col[2])
        bias = turned_rows[0:64, 3:4]
        for d in range(3):
            bias = bias + shift[d] * turned_rows[0:64, d : d + 1]
        f1[net, 0:64, :] = left(m1)
        b1h[net] = left(m1t)
        for d in range(3):
            f1[net, 64 * (d + 1) : 64 * (d + 2), :] = left(m1 * row[d])
            b1s[net, :, 192 * d : 192 * (d + 1)] = left(m1t * col[d])
        f1[net, 256:320, :] = left(m1 * square_row)
        b1p[net] = left(m1t * square_col)
        f2[net] = left(mats[:, 64:128])
        b2[net] = left(turned[64:128])
        lane = lax.broadcasted_iota(jnp.int32, (64, 8), 1)
        kept = turned_rows[0:64, 0:8]
        for d in range(3):
            kept = jnp.where(lane == d, col[d], kept)
        cols[net, :, 0:8] = jnp.where(lane == 3, bias, kept)

    xyz = points[...]
    lane_ones = jnp.ones((1, count), f32)
    xp[0:3, :] = xyz
    xp[3:4, :] = lane_ones
    xp[4:8, :] = jnp.zeros((4, count), f32)
    x_terms = three(xp[...])
    xpb[...] = jnp.zeros(xpb.shape, bf16)
    xpb[0:16, :] = jnp.concatenate([x_terms[0].astype(f32), x_terms[1].astype(f32)], 0).astype(bf16)

    def present(axis, facing):
        if facing < 0:
            return jnp.where(me[axis] > 0, 1.0, 0.0).astype(f32)
        return jnp.where(me[axis] < sizes[axis] - 1, 1.0, 0.0).astype(f32)

    inside = lane_ones
    curve = jnp.zeros((1, count), f32)
    for axis in range(3):
        along = xyz[axis : axis + 1]
        upper = along > 0.0
        facing = jnp.where(upper, 1.0, -1.0)
        depth = jnp.minimum((0.5 - jnp.abs(along)) * inverse_depth, 1.0)
        exists = jnp.where(upper, present(axis, 1), present(axis, -1))
        blend, slope, bend = window(depth, facing)
        inside = inside - exists * blend
        curve = curve - exists * bend
        alpha[2, 1 + axis : 2 + axis, :] = -2.0 * exists * slope
    alpha[2, 0:1, :] = wave_square * inside + curve
    alpha[2, 4:5, :] = inside
    for net in (0, 1):
        alpha[net, 0:1, :] = wave_square * lane_ones
        alpha[net, 1:4, :] = jnp.zeros((3, count), f32)
        alpha[net, 4:5, :] = lane_ones

    half = lax.broadcasted_iota(jnp.int32, (1, pair), 1) < slots
    point_id = lax.broadcasted_iota(jnp.int32, (count, pair), 0)
    stacked = jnp.concatenate([term.astype(f32) for term in x_terms], 0).astype(bf16)
    for axis in range(3):
        listed = jnp.concatenate([band[2 * axis : 2 * axis + 1, :], band[2 * axis + 1 : 2 * axis + 2, :]], 1)
        hot[axis] = jnp.where(point_id == listed, 1.0, 0.0).astype(bf16)
        taken = dot(stacked, hot[axis])
        taken = taken[0:8] + taken[8:16] + taken[16:24]
        xf[axis] = taken
        high, low = split(taken)
        xfb[axis] = jnp.zeros(xfb.shape[1:], bf16)
        xfb[axis, 0:16, :] = jnp.concatenate([high.astype(f32), low.astype(f32)], 0).astype(bf16)
        facing = jnp.where(half, -1.0, 1.0)
        exists = jnp.where(half, present(axis, -1), present(axis, 1))
        depth = jnp.minimum((0.5 - facing * taken[axis : axis + 1]) * inverse_depth, 1.0)
        blend, slope, bend = window(depth, facing)
        falpha[axis, 0:1, :] = exists * (wave_square * blend + bend)
        falpha[axis, 1:4, :] = jnp.zeros((3, pair), f32)
        falpha[axis, 1 + axis : 2 + axis, :] = 2.0 * exists * slope
        falpha[axis, 4:5, :] = exists * blend

    def tanh_layer(z, f, m):
        h = jnp.tanh(z)
        s = 1.0 - h * h
        q = f[0] * f[0] + f[1] * f[1] + f[2] * f[2]
        return h, s, q, m - 2.0 * h * q

    def forward(get, x, al, mm, keep0, keep1, keep2):
        z = get(0) * x[0:1] + get(1) * x[1:2] + get(2) * x[2:3] + get(3)
        h = jnp.tanh(z)
        s = 1.0 - h * h
        p = h * s
        parts = [split(v) for v in (h, s, p)]
        keep0(h, parts)
        m1h = mm(f1, 0, 64, right(*parts[0]))
        m1f = mm(f1, 64, 256, right(*parts[1]))
        m1l = mm(f1, 256, 320, right(*parts[2]))
        f = [m1f[64 * d : 64 * (d + 1)] for d in range(3)]
        h, s, q, w = tanh_layer(m1h + get(4), f, m1l)
        parts = [split(v) for v in (h, s * f[0], s * f[1], s * f[2], s * w)]
        keep1(h, f, q, w, parts)
        n = x.shape[1]
        out = mm(f2, 0, 64, jnp.concatenate([right(*part) for part in parts], 1))
        out = [out[:, n * k : n * (k + 1)] for k in range(5)]
        f = out[1:4]
        h, s, q, w = tanh_layer(out[0] + get(5), f, out[4])
        u = al[1:2] * f[0] + al[2:3] * f[1] + al[3:4] * f[2] + al[4:5] * w
        c = al[0:1] * h + s * u
        keep2(h, f, q, u, c)
        return jnp.sum(get(6) * c, axis=0, keepdims=True)

    def backward(get, al, delta, mm, lane_sum, saved0, saved1, saved2):
        h, fa, fb, fc, q, u, c = saved2
        f = (fa, fb, fc)
        dlast = lane_sum(delta * c)
        e = get(6) * delta
        s = 1.0 - h * h
        es = e * s
        gm = es * al[4:5]
        k = 4.0 * h * gm
        gf = [es * al[1 + d : 2 + d] - k * f[d] for d in range(3)]
        gz = (e * al[0:1] - 2.0 * (q * gm + h * (e * u))) * s
        dbias1 = lane_sum(gz)
        g2 = [split(v) for v in (gz, gf[0], gf[1], gf[2], gm)]
        out = mm(b2, 0, 64, jnp.concatenate([right(*part) for part in g2], 1))
        n = e.shape[1]
        oh, oa, ob, oc, ol = [out[:, n * k : n * (k + 1)] for k in range(5)]
        o = (oa, ob, oc)
        h, fa, fb, fc, q, w = saved1
        f = (fa, fb, fc)
        s = 1.0 - h * h
        gm = ol * s
        k = 4.0 * h * gm
        gf = [o[d] * s - k * f[d] for d in range(3)]
        gs = o[0] * f[0] + o[1] * f[1] + o[2] * f[2] + ol * w
        gz = (oh - 2.0 * (q * gm + h * gs)) * s
        dbias0 = lane_sum(gz)
        g1 = [split(v) for v in (gz, gf[0], gf[1], gf[2], gm)]
        oh = mm(b1h, 0, 64, right(*g1[0]))
        os = mm(b1s, 0, 64, jnp.concatenate([right(*part) for part in g1[1:4]], 0))
        op = mm(b1p, 0, 64, right(*g1[4]))
        h = saved0
        s = 1.0 - h * h
        gz = (oh + op * s - 2.0 * h * (os + op * h)) * s
        return g2, g1, split(gz), dlast, dbias1, dbias0

    def fold(product):
        return product[0:64] + product[64:128]

    def finish(net, scale, shift, dm2, ah, af, al, pts, dlast, dbias1, dbias0, extra):
        lane = lax.broadcasted_iota(jnp.int32, (64, 128), 1)
        pts = jnp.where(lane == 4, dbias0, pts)
        pts = jnp.where(lane == 5, dbias1, pts)
        pts = jnp.where(lane == 6, dlast, pts)
        turned = pts.T
        sums = turned[0:8] + turned[8:16]
        m1 = nets[net, 0:64, 0:64]
        rows = nets[net, 64:72, 0:64]
        row = [scale[d] * rows[d : d + 1] for d in range(3)]
        square = row[0] * row[0] + row[1] * row[1] + row[2] * row[2]
        dsquare = -2.0 * jnp.sum(m1 * al, axis=0, keepdims=True)
        dm1 = ah - 2.0 * (al * square)
        first = []
        for d in range(3):
            dm1 = dm1 + af[d] * row[d]
            slope = sums[d : d + 1] + jnp.sum(m1 * af[d], axis=0, keepdims=True) + 2.0 * row[d] * dsquare
            first.append(scale[d] * slope + shift[d] * sums[3:4])
        grads[net, 0:64, :] = jnp.concatenate([dm1, dm2], 1)
        grads[net, 64:72, 0:64] = jnp.concatenate(first + [sums[3:7], extra], 0)
        grads[net, 64:72, 64:128] = jnp.zeros((8, 64), f32)

    def row_sums(value):
        return jnp.sum(value, axis=1, keepdims=True)

    def half_sums(value):
        return row_sums(jnp.where(half, value, 0.0)), row_sums(jnp.where(half, 0.0, value))

    def forward_wide(net):
        def get(k):
            return cols[net, :, k : k + 1]

        def mm(ref, low, high, rhs):
            return dot(ref[net, low:high, :], rhs)

        for start in range(0, count, chunk):
            span = slice(start, start + chunk)

            def keep0(h, parts):
                h0s[net, :, span] = h
                for k, part in enumerate(parts):
                    x0[net, k, 0:64, span] = part[0]
                    x0[net, k, 64:128, span] = part[1]

            def keep1(h, f, q, w, parts):
                for k, value in enumerate((h, f[0], f[1], f[2], q, w)):
                    a1[net, k, :, span] = value
                for k, part in enumerate(parts):
                    x1[net, k, 0:64, span] = part[0]
                    x1[net, k, 64:128, span] = part[1]

            def keep2(h, f, q, u, c):
                for k, value in enumerate((h, f[0], f[1], f[2], q, u, c)):
                    a2[net, k, :, span] = value

            row = forward(get, xp[:, span], alpha[net, :, span], mm, keep0, keep1, keep2)
            res[0:1, span] = res[0:1, span] + row

    def backward_wide(net, extra):
        def get(k):
            return cols[net, :, k : k + 1]

        def mm(ref, low, high, rhs):
            return dot(ref[net, low:high, :], rhs)

        g2, g1, g0, sums = [], [], [], None
        for start in range(0, count, chunk):
            span = slice(start, start + chunk)
            part = backward(
                get,
                alpha[net, :, span],
                res[1:2, span],
                mm,
                row_sums,
                h0s[net, :, span],
                [a1[net, k, :, span] for k in range(6)],
                [a2[net, k, :, span] for k in range(7)],
            )
            g2.append(part[0])
            g1.append(part[1])
            g0.append(part[2])
            sums = part[3:] if sums is None else tuple(a + b for a, b in zip(sums, part[3:]))

        def stack(pieces):
            return jnp.concatenate([jnp.concatenate(piece, 0) for piece in pieces], 1)

        lhs = jnp.concatenate([stack([g[k] for g in g2]) for k in range(5)], 1)
        rhs = jnp.concatenate([x1[net, k] for k in range(5)], 1)
        dm2 = fold(dot_nt(lhs, rhs))
        ah = fold(dot_nt(stack([g[0] for g in g1]), x0[net, 0]))
        lhs = jnp.concatenate([stack([g[1 + d] for g in g1]) for d in range(3)], 0)
        af = dot_nt(lhs, x0[net, 1])
        al = fold(dot_nt(stack([g[4] for g in g1]), x0[net, 2]))
        pts = fold(dot_nt(stack(g0), xpb[...]))
        af = [fold(af[128 * d : 128 * (d + 1)]) for d in range(3)]

        def sides(value):
            return value[:, 0:64] + value[:, 64:128]

        scale, shift = affine(net)
        finish(net, scale, shift, sides(dm2), sides(ah), [sides(v) for v in af], sides(al), pts, *sums, extra)

    wide_half = (lax.broadcasted_iota(jnp.int32, (1, 5 * pair), 1) & (pair - 1)) < slots

    def pair_tools(axis):
        net = 3 + 2 * axis

        def get(k):
            return jnp.where(half, cols[net, :, k : k + 1], cols[net + 1, :, k : k + 1])

        def mm(ref, low, high, rhs):
            rows = high - low
            lhs = jnp.concatenate([ref[net, low:high, :], ref[net + 1, low:high, :]], 0)
            out = dot(lhs, rhs)
            return jnp.where(wide_half[:, 0 : rhs.shape[1]], out[0:rows], out[rows : 2 * rows])

        return net, get, mm

    first_half = jnp.where(half, 1.0, 0.0).astype(bf16)
    second_half = jnp.where(half, 0.0, 1.0).astype(bf16)

    def forward_pair(axis):
        net, get, mm = pair_tools(axis)

        def keep_parts(ref, parts):
            for k, part in enumerate(parts):
                ref[axis, k, 0:64, :] = part[0] * first_half
                ref[axis, k, 64:128, :] = part[1] * first_half
                ref[axis, k, 128:192, :] = part[0] * second_half
                ref[axis, k, 192:256, :] = part[1] * second_half

        def keep0(h, parts):
            fh0s[axis] = h
            keep_parts(fx0, parts)

        def keep1(h, f, q, w, parts):
            for k, value in enumerate((h, f[0], f[1], f[2], q, w)):
                fa1[axis, k] = value
            keep_parts(fx1, parts)

        def keep2(h, f, q, u, c):
            for k, value in enumerate((h, f[0], f[1], f[2], q, u, c)):
                fa2[axis, k] = value

        row = forward(get, xf[axis], falpha[axis], mm, keep0, keep1, keep2)
        terms = jnp.concatenate([term.astype(f32) for term in three(row)] + [jnp.zeros((5, pair), f32)], 0)
        spread = dot_nt(terms.astype(bf16), hot[axis])
        res[0:1, :] = res[0:1, :] + (spread[0:1] + spread[1:2] + spread[2:3])

    def backward_pair(axis):
        net, get, mm = pair_tools(axis)
        delta = fdelta[axis, 0:1, :]
        al = falpha[axis]
        g2, g1, g0, dlast, dbias1, dbias0 = backward(
            get,
            al,
            delta,
            mm,
            half_sums,
            fh0s[axis],
            [fa1[axis, k] for k in range(6)],
            [fa2[axis, k] for k in range(7)],
        )

        def stack(piece):
            return jnp.concatenate(piece, 0)

        dm2 = fold(
            dot_nt(
                jnp.concatenate([stack(g) for g in g2], 1),
                jnp.concatenate([fx1[axis, k] for k in range(5)], 1),
            )
        )
        ah = fold(dot_nt(stack(g1[0]), fx0[axis, 0]))
        af = dot_nt(jnp.concatenate([stack(g1[1 + d]) for d in range(3)], 0), fx0[axis, 1])
        af = [fold(af[128 * d : 128 * (d + 1)]) for d in range(3)]
        al = fold(dot_nt(stack(g1[4]), fx0[axis, 2]))
        points_here = xfb[axis]
        for side in range(2):
            kept = first_half if side == 0 else second_half
            pts = fold(dot_nt(stack(g0), points_here * kept))

            def sides(value):
                return value[:, 128 * side : 128 * side + 64] + value[:, 128 * side + 64 : 128 * side + 128]

            scale = [2.0, 2.0, 2.0]
            shift = [jnp.where(axis == d, 2.0 - 4.0 * side, 0.0) for d in range(3)]
            finish(
                net + side,
                scale,
                shift,
                sides(dm2),
                sides(ah),
                [sides(v) for v in af],
                sides(al),
                pts,
                dlast[side],
                dbias1[side],
                dbias0[side],
                jnp.zeros((1, 64), f32),
            )

    def spread_out(axis, source_of, ref, send, recv):
        for offset in range(1, sizes[axis]):
            target = lax.rem(me[axis] + offset, sizes[axis])
            pltpu.make_async_remote_copy(
                src_ref=source_of(target),
                dst_ref=ref.at[me[axis]],
                send_sem=send.at[offset],
                recv_sem=recv.at[me[axis]],
                device_id=peer(axis, offset),
                device_id_type=MESH,
            ).start()

    def collect(axis, source_of, ref, send, recv):
        for offset in range(1, sizes[axis]):
            target = lax.rem(me[axis] + offset, sizes[axis])
            sender = lax.rem(me[axis] + (sizes[axis] - offset), sizes[axis])
            copy = pltpu.make_async_remote_copy(
                src_ref=source_of(target),
                dst_ref=ref.at[sender],
                send_sem=send.at[offset],
                recv_sem=recv.at[sender],
                device_id=peer(axis, offset),
                device_id_type=MESH,
            )
            copy.wait()

    def total(ref, number):
        value = ref[0]
        for k in range(1, number):
            value = value + ref[k]
        return value

    def chunked(ref, net):
        rows = 64 // sizes[2]
        for k in range(sizes[2]):
            ref[k, 0:rows, :] = grads[net, rows * k : rows * (k + 1), :]
            ref[k, rows : rows + 8 // sizes[2], :] = grads[net, 64 + 8 // sizes[2] * k : 64 + 8 // sizes[2] * (k + 1), :]

    def unchunk(ref, first_ref, mid_ref, last_ref, loss_ref):
        rows = 64 // sizes[2]
        extras = []
        for k in range(sizes[2]):
            block = ref[k]
            mid_ref[0, rows * k : rows * (k + 1), :] = block[0:rows, 0:64]
            mid_ref[1, rows * k : rows * (k + 1), :] = block[0:rows, 64:128]
            extras.append(block[rows : rows + 8 // sizes[2], 0:64])
        extras = jnp.concatenate(extras, 0)
        first_ref[...] = extras[0:4]
        last_ref[...] = extras[4:7]
        if loss_ref is not None:
            loss_ref[...] = extras[7:8, 0:1]

    g_rs = (2, lambda target: gchunks.at[target], grs, grs_send, grs_recv)
    c_rs = (2, lambda target: cchunks.at[target], crs, crs_send, crs_recv)
    g_y = (1, lambda target: gys.at[me[1]], gys, gy_send, gy_recv)
    g_x = (0, lambda target: gxs.at[me[0]], gxs, gx_send, gx_recv)
    g_ag = (2, lambda target: gag.at[me[2]], gag, gag_send, gag_recv)
    c_ag = (2, lambda target: cag.at[me[2]], cag, cag_send, cag_recv)

    def send_back(face):
        axis, up = face // 2, face % 2
        return pltpu.make_async_remote_copy(
            src_ref=grads.at[3 + face],
            dst_ref=back.at[face ^ 1],
            send_sem=back_send.at[face],
            recv_sem=back_recv.at[face ^ 1],
            device_id=peer(axis, 2 * up - 1),
            device_id_type=MESH,
        )

    res[0:1, :] = -source[...]

    def prepare_wide(net, carry):
        prepare(net, *affine(net))
        forward_wide(net)
        return carry

    lax.fori_loop(0, 3, prepare_wide, 0)
    gchunks[...] = jnp.zeros(gchunks.shape, f32)
    cchunks[...] = jnp.zeros(cchunks.shape, f32)

    for face in range(6):
        halo(face).wait()

    def face_shift(axis, side):
        return [jnp.where(axis == d, 2.0 - 4.0 * side, 0.0) for d in range(3)]

    def forward_faces(axis, carry):
        for side in range(2):
            prepare(3 + 2 * axis + side, [2.0, 2.0, 2.0], face_shift(axis, side))
        forward_pair(axis)
        return carry

    lax.fori_loop(0, 3, forward_faces, 0)

    residual = res[0:1, :]
    residual_out[...] = residual
    delta = residual * (1.0 / count)
    res[1:2, :] = delta
    loss = jnp.sum(residual * residual, axis=1, keepdims=True) * (0.5 / count)
    terms = jnp.concatenate([term.astype(f32) for term in three(delta)] + [jnp.zeros((5, count), f32)], 0)
    terms = terms.astype(bf16)
    for axis in range(3):
        taken = dot(terms, hot[axis])
        fdelta[axis, 0:1, :] = taken[0:1] + taken[1:2] + taken[2:3]

    first_lane = lax.broadcasted_iota(jnp.int32, (1, 64), 1) == 0

    def backward_two(net, carry):
        extra = jnp.where(first_lane & (net == 0), loss, 0.0)
        backward_wide(net, extra)
        return carry

    lax.fori_loop(0, 2, backward_two, 0)
    chunked(gchunks, 0)
    chunked(cchunks, 1)
    grs[me[2]] = gchunks[me[2]]
    crs[me[2]] = cchunks[me[2]]
    spread_out(*g_rs)
    spread_out(*c_rs)

    def backward_faces(axis, carry):
        backward_pair(axis)
        return carry

    lax.fori_loop(0, 3, backward_faces, 0)
    for face in range(6):
        send_back(face).start()

    collect(*g_rs)
    gys[me[1]] = total(grs, sizes[2])
    spread_out(*g_y)
    collect(*c_rs)
    cag[me[2]] = total(crs, sizes[2])
    spread_out(*c_ag)

    backward_wide(2, jnp.zeros((1, 64), f32))

    collect(*g_y)
    gxs[me[0]] = total(gys, sizes[1])
    spread_out(*g_x)
    collect(*c_ag)
    unchunk(cag, column_first_out, column_mid_out, column_last_out, None)
    for face in range(6):
        send_back(face).wait()
    collect(*g_x)
    gag[me[2]] = total(gxs, sizes[0])
    spread_out(*g_ag)
    fine = grads[2] + total(back, 6)
    fine_mid_out[0] = fine[0:64, 0:64]
    fine_mid_out[1] = fine[0:64, 64:128]
    fine_first_out[...] = fine[64:68, 0:64]
    fine_last_out[...] = fine[68:71, 0:64]
    collect(*g_ag)
    unchunk(gag, global_first_out, global_mid_out, global_last_out, loss_out)


def step(sizes, points, band_index, source, *params):
    count = points.shape[-1]
    slots = band_index.shape[-1]
    chunk = 256
    pair = 2 * slots
    shapes = [(4, 64), (2, 64, 64), (3, 64)]
    operands = [points.reshape(3, count), band_index.reshape(6, slots), source.reshape(1, count)]
    operands += [param.reshape(shapes[k % 3]) for k, param in enumerate(params)]
    outs = [(1, count)] + shapes * 3 + [(1, 1)]
    vmem = pltpu.VMEM
    block = 16 * max(1, 8 // sizes[2])
    scratch = [
        vmem((9, 72, 128), f32),
        vmem((9, 72, 128), f32),
        vmem((9, 320, 192), bf16),
        vmem((9, 64, 192), bf16),
        vmem((9, 64, 192), bf16),
        vmem((9, 64, 192), bf16),
        vmem((9, 64, 576), bf16),
        vmem((9, 64, 192), bf16),
        vmem((9, 64, 128), f32),
        vmem((8, count), f32),
        vmem((128, count), bf16),
        vmem((3, 8, count), f32),
        vmem((3, 3, 128, count), bf16),
        vmem((3, 5, 128, count), bf16),
        vmem((3, 64, count), f32),
        vmem((3, 6, 64, count), f32),
        vmem((3, 7, 64, count), f32),
        vmem((8, count), f32),
        vmem((3, 8, pair), f32),
        vmem((3, 128, pair), bf16),
        vmem((3, 8, pair), f32),
        vmem((3, 3, 256, pair), bf16),
        vmem((3, 5, 256, pair), bf16),
        vmem((3, 64, pair), f32),
        vmem((3, 6, 64, pair), f32),
        vmem((3, 7, 64, pair), f32),
        vmem((3, 8, pair), f32),
        vmem((3, count, pair), bf16),
        vmem((6, 72, 128), f32),
        vmem((sizes[2], block, 128), f32),
        vmem((sizes[2], block, 128), f32),
        vmem((sizes[2], block, 128), f32),
        vmem((sizes[1], block, 128), f32),
        vmem((sizes[0], block, 128), f32),
        vmem((sizes[2], block, 128), f32),
        vmem((sizes[2], block, 128), f32),
        vmem((sizes[2], block, 128), f32),
    ]
    dma = pltpu.SemaphoreType.DMA
    scratch += [dma((6,))] * 4
    scratch += [dma((sizes[k],)) for k in (2, 2, 1, 1, 0, 0, 2, 2, 2, 2, 2, 2)]
    whole = pl.BlockSpec(memory_space=pltpu.VMEM)
    results = pl.pallas_call(
        functools.partial(kernel, sizes, chunk),
        out_shape=[jax.ShapeDtypeStruct(shape, f32) for shape in outs],
        in_specs=[whole] * 12,
        out_specs=[whole] * 11,
        scratch_shapes=scratch,
        compiler_params=pltpu.CompilerParams(
            collective_id=0, has_side_effects=True, vmem_limit_bytes=40 << 20
        ),
        cost_estimate=pl.CostEstimate(flops=500_000_000, bytes_accessed=1_000_000, transcendentals=400_000),
        name="training_step",
    )(*operands)
    lead = [(1, 1, 1)] * 4 + [(1, 1)] * 3 + [()] * 3
    arrays = [results[0].reshape(1, 1, 1, count)]
    arrays += [value.reshape(front + value.shape) for value, front in zip(results[1:10], lead[1:])]
    return tuple(arrays) + (results[10].reshape(()),)


def solution(mesh):
    sizes = tuple(mesh.shape[axis] for axis in AXES)
    cell = ("gx", "gy", "gz")
    column = ("gx", "gy")
    in_specs = (P(*cell, None, None), P(*cell, None, None), P(*cell, None))
    nets_specs = (
        (P(*cell, None, None), P(*cell, None, None, None), P(*cell, None, None))
        + (P(*column, None, None), P(*column, None, None, None), P(*column, None, None))
        + (P(), P(), P())
    )
    return jax.shard_map(
        functools.partial(step, sizes),
        mesh=mesh,
        in_specs=in_specs + nets_specs,
        out_specs=(P(*cell, None),) + nets_specs + (P(),),
        check_vma=False,
    )
```

```python
import functools

import jax
import jax.numpy as jnp
from jax import lax
from jax.experimental import pallas as pl
from jax.experimental.pallas import tpu as pltpu
from jax.sharding import PartitionSpec as P

MESH = pl.DeviceIdType.MESH
AXES = ("gx", "gy", "gz")
f32, bf16 = jnp.float32, jnp.bfloat16
wave_square = 4.0
inverse_depth = 8.0
TILES = 9
NT = (((1,), (1,)), ((), ()))


def split(value):
    high = value.astype(bf16)
    return high, (value - high.astype(f32)).astype(bf16)


def three(value):
    first = value.astype(bf16)
    rest = value - first.astype(f32)
    second = rest.astype(bf16)
    return first, second, (rest - second.astype(f32)).astype(bf16)


def left(matrix):
    high = matrix.astype(bf16).astype(f32)
    return jnp.concatenate([high, high, matrix - high], 1).astype(bf16)


def right(high, low):
    return jnp.concatenate([high, low, high], 0)


def dot(a, b):
    return jnp.dot(a, b, preferred_element_type=f32)


def dot_nt(a, b):
    return lax.dot_general(a, b, NT, preferred_element_type=f32)


def window(depth, facing):
    square = depth * depth
    smooth = depth * (15.0 - 10.0 * square + 3.0 * square * square) / 8.0
    blend = 0.5 * (1.0 - smooth)
    slope = (0.5 * inverse_depth * 15.0 / 8.0) * facing * (1.0 - square) * (1.0 - square)
    bend = (0.5 * inverse_depth * inverse_depth * 7.5) * depth * (1.0 - square)
    return blend, slope, bend


def kernel(sizes, *refs):
    (
        points_hbm,
        band_hbm,
        source_hbm,
        fine_first_hbm,
        fine_mid_hbm,
        fine_last_hbm,
        column_first_hbm,
        column_mid_hbm,
        column_last_hbm,
        global_first_hbm,
        global_mid_hbm,
        global_last_hbm,
        residual_out,
        fine_first_out,
        fine_mid_out,
        fine_last_out,
        column_first_out,
        column_mid_out,
        column_last_out,
        global_first_out,
        global_mid_out,
        global_last_out,
        loss_out,
        points,
        band,
        source,
        fine_first,
        fine_mid,
        fine_last,
        column_first,
        column_mid,
        column_last,
        global_first,
        global_mid,
        global_last,
        nets,
        grads,
        f1,
        f2,
        b2,
        b1h,
        b1s,
        b1p,
        cols,
        xp,
        xpb,
        alpha,
        x0,
        x1,
        h0s,
        a1,
        a2,
        res,
        xf,
        xfb,
        falpha,
        fcols,
        fx0,
        fx1,
        fh0s,
        fa1,
        fa2,
        fdelta,
        hot,
        back,
        tiles,
        levels,
        summed,
        columns,
        load_sem,
        halo_send,
        halo_recv,
        back_send,
        back_recv,
        tile_send,
        tile_recv,
        level_send,
        level_recv,
        share_send,
        share_recv,
        column_send,
        column_recv,
    ) = refs
    me = tuple(lax.axis_index(axis) for axis in AXES)
    count = points.shape[2]
    slots = band.shape[2]
    pair = 2 * slots
    near = 6 * slots
    plane = sizes[0] * sizes[1]
    stride = plane // TILES
    here = me[0] * sizes[1] + me[1]
    reducer = (lax.rem(here, stride) == 0) & (here // stride < TILES)
    my_rows = pl.ds(pl.multiple_of(8 * lax.rem(here // stride, TILES), 8), 8)

    def peer(axis, offset):
        other = list(me)
        other[axis] = lax.rem(me[axis] + (offset + sizes[axis]), sizes[axis])
        return tuple(other)

    def in_plane(place):
        return (place // sizes[1], lax.rem(place, sizes[1]), me[2])

    barrier = pltpu.get_barrier_semaphore()
    friends = [in_plane(lax.rem(here + offset, plane)) for offset in range(1, plane)]
    friends += [peer(2, offset) for offset in range(1, sizes[2])]
    for friend in friends:
        pl.semaphore_signal(barrier, inc=1, device_id=friend, device_id_type=MESH)

    loads = [
        pltpu.make_async_copy(refs[k], refs[23 + k], load_sem.at[k])
        for k in (4, 3, 5, 0, 1, 2, 10, 9, 11, 7, 6, 8)
    ]
    for load in loads:
        load.start()

    def pack(net, first, mid, last):
        nets[net, 0:64, :] = jnp.concatenate([mid[0], mid[1]], 1)
        nets[net, 64:68, 0:64] = first[...]
        for k in range(3):
            nets[net, 68 + k : 69 + k, 0:64] = last[k] if len(last.shape) == 3 else last[k : k + 1, :]
        nets[net, 71:72, 0:64] = jnp.zeros((1, 64), f32)
        nets[net, 64:72, 64:128] = jnp.zeros((8, 64), f32)

    for load in loads[:3]:
        load.wait()
    pack(2, fine_first, fine_mid, fine_last)
    for load in loads[3:]:
        load.wait()
    pack(1, column_first, column_mid, column_last)
    pack(0, global_first, global_mid, global_last)

    def halo(face):
        axis, up = face // 2, face % 2
        return pltpu.make_async_remote_copy(
            src_ref=nets.at[2],
            dst_ref=nets.at[3 + (face ^ 1)],
            send_sem=halo_send.at[face],
            recv_sem=halo_recv.at[face ^ 1],
            device_id=peer(axis, 2 * up - 1),
            device_id_type=MESH,
        )

    faces = [face for face in range(6) if sizes[face // 2] > 1]
    place = [me[axis].astype(f32) for axis in range(3)]

    def affine(net):
        scale, shift = [], []
        for axis in range(3):
            fitted_scale = 2.0 / sizes[axis]
            fitted_shift = (2.0 * place[axis] + 1.0) * (1.0 / sizes[axis]) - 1.0
            fitted = (net == 0) if axis < 2 else (net <= 1)
            scale.append(jnp.where(fitted, fitted_scale, 2.0))
            shift.append(jnp.where(fitted, fitted_shift, 0.0))
        return scale, shift

    def face_affine(face):
        shift = [0.0, 0.0, 0.0]
        shift[face // 2] = 2.0 - 4.0 * (face % 2)
        return [2.0, 2.0, 2.0], shift

    def prepare_forward(net, scale, shift):
        mats = nets[net, 0:64, :]
        rows = nets[net, 64:72, :]
        turned = rows.T
        m1 = mats[:, 0:64]
        row = [scale[d] * rows[d : d + 1, 0:64] for d in range(3)]
        square = -2.0 * (row[0] * row[0] + row[1] * row[1] + row[2] * row[2])
        bias = turned[0:64, 3:4]
        for d in range(3):
            bias = bias + shift[d] * turned[0:64, d : d + 1]
        f1[net, 0:64, :] = left(m1)
        for d in range(3):
            f1[net, 64 * (d + 1) : 64 * (d + 2), :] = left(m1 * row[d])
        f1[net, 256:320, :] = left(m1 * square)
        f2[net] = left(mats[:, 64:128])
        lane = lax.broadcasted_iota(jnp.int32, (64, 8), 1)
        kept = turned[0:64, 0:8]
        for d in range(3):
            kept = jnp.where(lane == d, scale[d] * kept, kept)
        cols[net, :, 0:8] = jnp.where(lane == 3, bias, kept)

    def prepare_backward(net):
        turned = nets[net, 0:64, :].T
        m1t = turned[0:64]
        b1h[net] = left(m1t)
        col = [cols[net, :, d : d + 1] for d in range(3)]
        for d in range(3):
            b1s[net, :, 192 * d : 192 * (d + 1)] = left(m1t * col[d])
        b1p[net] = left(m1t * (-2.0 * (col[0] * col[0] + col[1] * col[1] + col[2] * col[2])))
        b2[net] = left(turned[64:128])

    lane_ones = jnp.ones((1, count), f32)
    for d in range(3):
        xp[d : d + 1, :] = points[d]
    xp[3:4, :] = lane_ones
    xp[4:8, :] = jnp.zeros((4, count), f32)
    x_terms = three(xp[...])
    xpb[...] = jnp.zeros(xpb.shape, bf16)
    xpb[0:16, :] = jnp.concatenate([x_terms[0].astype(f32), x_terms[1].astype(f32)], 0).astype(bf16)

    def present(face):
        axis = face // 2
        there = me[axis] < sizes[axis] - 1 if face % 2 else me[axis] > 0
        return jnp.where(there, 1.0, 0.0).astype(f32)

    inside = lane_ones
    curve = jnp.zeros((1, count), f32)
    for axis in range(3):
        along = points[axis]
        upper = along > 0.0
        facing = jnp.where(upper, 1.0, -1.0)
        depth = jnp.minimum((0.5 - jnp.abs(along)) * inverse_depth, 1.0)
        exists = jnp.where(upper, present(2 * axis + 1), present(2 * axis))
        blend, slope, bend = window(depth, facing)
        inside = inside - exists * blend
        curve = curve - exists * bend
        alpha[2, 1 + axis : 2 + axis, :] = -2.0 * exists * slope
    alpha[2, 0:1, :] = wave_square * inside + curve
    alpha[2, 4:5, :] = inside
    for net in (0, 1):
        alpha[net, 0:1, :] = wave_square * lane_ones
        alpha[net, 1:4, :] = jnp.zeros((3, count), f32)
        alpha[net, 4:5, :] = lane_ones

    if friends:
        pl.semaphore_wait(barrier, len(friends))
    for face in faces:
        halo(face).start()

    near_lane = lax.broadcasted_iota(jnp.int32, (1, near), 1)
    face_of = near_lane // slots
    lower = lax.rem(face_of, 2) == 0
    stacked = jnp.concatenate([term.astype(f32) for term in x_terms], 0).astype(bf16)
    point_id = lax.broadcasted_iota(jnp.int32, (count, near), 0)
    listed = jnp.concatenate([band[face] for face in range(6)], 1)
    hot[...] = jnp.where(point_id == listed, 1.0, 0.0).astype(bf16)
    taken = dot(stacked, hot[...])
    taken = taken[0:8] + taken[8:16] + taken[16:24]
    xf[...] = taken
    high, low = split(taken)
    xfb[...] = jnp.zeros(xfb.shape, bf16)
    xfb[0:16, :] = jnp.concatenate([high.astype(f32), low.astype(f32)], 0).astype(bf16)
    facing = jnp.where(lower, -1.0, 1.0)
    axis_of = face_of // 2
    along = jnp.where(axis_of == 0, taken[0:1], jnp.where(axis_of == 1, taken[1:2], taken[2:3]))
    exists = jnp.zeros((1, near), f32)
    for face in range(6):
        exists = jnp.where(face_of == face, present(face), exists)
    depth = jnp.minimum((0.5 - facing * along) * inverse_depth, 1.0)
    blend, slope, bend = window(depth, facing)
    falpha[0:1, :] = exists * (wave_square * blend + bend)
    for d in range(3):
        falpha[1 + d : 2 + d, :] = jnp.where(axis_of == d, 2.0 * exists * slope, 0.0)
    falpha[4:5, :] = exists * blend

    def tanh_layer(z, f, m):
        h = jnp.tanh(z)
        s = 1.0 - h * h
        q = f[0] * f[0] + f[1] * f[1] + f[2] * f[2]
        return h, s, q, m - 2.0 * h * q

    def forward(get, x, al, mm, keep0, keep1, keep2):
        z = get(0) * x[0:1] + get(1) * x[1:2] + get(2) * x[2:3] + get(3)
        h = jnp.tanh(z)
        s = 1.0 - h * h
        p = h * s
        parts = [split(v) for v in (h, s, p)]
        keep0(h, parts)
        m1h = mm(f1, 0, 64, [right(*parts[0])])[0]
        m1f = mm(f1, 64, 256, [right(*parts[1])])[0]
        m1l = mm(f1, 256, 320, [right(*parts[2])])[0]
        f = [m1f[64 * d : 64 * (d + 1)] for d in range(3)]
        h, s, q, w = tanh_layer(m1h + get(4), f, m1l)
        parts = [split(v) for v in (h, s * f[0], s * f[1], s * f[2], s * w)]
        keep1((h, f[0], f[1], f[2], q, w), parts)
        out = mm(f2, 0, 64, [right(*part) for part in parts])
        f = out[1:4]
        h, s, q, w = tanh_layer(out[0] + get(5), f, out[4])
        u = al[1:2] * f[0] + al[2:3] * f[1] + al[3:4] * f[2] + al[4:5] * w
        c = al[0:1] * h + s * u
        keep2((h, f[0], f[1], f[2], q, u, c))
        return jnp.sum(get(6) * c, axis=0, keepdims=True)

    def backward(get, al, delta, mm, lane_sum, saved0, saved1, saved2):
        h, fa, fb, fc, q, u, c = saved2
        f = (fa, fb, fc)
        dlast = lane_sum(delta * c)
        e = get(6) * delta
        s = 1.0 - h * h
        es = e * s
        gm = es * al[4:5]
        k = 4.0 * h * gm
        gf = [es * al[1 + d : 2 + d] - k * f[d] for d in range(3)]
        gz = (e * al[0:1] - 2.0 * (q * gm + h * (e * u))) * s
        dbias1 = lane_sum(gz)
        g2 = [split(v) for v in (gz, gf[0], gf[1], gf[2], gm)]
        oh, oa, ob, oc, ol = mm(b2, 0, 64, [right(*part) for part in g2])
        o = (oa, ob, oc)
        h, fa, fb, fc, q, w = saved1
        f = (fa, fb, fc)
        s = 1.0 - h * h
        gm = ol * s
        k = 4.0 * h * gm
        gf = [o[d] * s - k * f[d] for d in range(3)]
        gs = o[0] * f[0] + o[1] * f[1] + o[2] * f[2] + ol * w
        gz = (oh - 2.0 * (q * gm + h * gs)) * s
        dbias0 = lane_sum(gz)
        g1 = [split(v) for v in (gz, gf[0], gf[1], gf[2], gm)]
        oh = mm(b1h, 0, 64, [right(*g1[0])])[0]
        os = mm(b1s, 0, 64, [jnp.concatenate([right(*part) for part in g1[1:4]], 0)])[0]
        op = mm(b1p, 0, 64, [right(*g1[4])])[0]
        h = saved0
        s = 1.0 - h * h
        gz = (oh + op * s - 2.0 * h * (os + op * h)) * s
        return g2, g1, split(gz), dlast, dbias1, dbias0

    def fold(product):
        return product[0:64] + product[64:128]

    def finish(net, scale, shift, dm2, ah, af, al, pts, dlast, dbias1, dbias0, extra):
        lane = lax.broadcasted_iota(jnp.int32, (64, 128), 1)
        pts = jnp.where(lane == 4, dbias0, pts)
        pts = jnp.where(lane == 5, dbias1, pts)
        pts = jnp.where(lane == 6, dlast, pts)
        turned = pts.T
        sums = turned[0:8] + turned[8:16]
        m1 = nets[net, 0:64, 0:64]
        rows = nets[net, 64:72, 0:64]
        row = [scale[d] * rows[d : d + 1] for d in range(3)]
        square = row[0] * row[0] + row[1] * row[1] + row[2] * row[2]
        dsquare = -2.0 * jnp.sum(m1 * al, axis=0, keepdims=True)
        dm1 = ah - 2.0 * (al * square)
        first = []
        for d in range(3):
            dm1 = dm1 + af[d] * row[d]
            slope = sums[d : d + 1] + jnp.sum(m1 * af[d], axis=0, keepdims=True) + 2.0 * row[d] * dsquare
            first.append(scale[d] * slope + shift[d] * sums[3:4])
        grads[net, 0:64, :] = jnp.concatenate([dm1, dm2], 1)
        grads[net, 64:72, 0:64] = jnp.concatenate(first + [sums[3:7], extra], 0)
        grads[net, 64:72, 64:128] = jnp.zeros((8, 64), f32)

    def wide_tools(net):
        def get(k):
            return cols[net, :, k : k + 1]

        def mm(ref, low, high, streams):
            out = dot(ref[net, low:high, :], jnp.concatenate(streams, 1))
            return [out[:, count * k : count * (k + 1)] for k in range(len(streams))]

        return get, mm

    def row_sums(value):
        return jnp.sum(value, axis=1, keepdims=True)

    def forward_wide(net):
        get, mm = wide_tools(net)

        def keep_parts(ref, parts):
            for k, part in enumerate(parts):
                ref[net, k, 0:64, :] = part[0]
                ref[net, k, 64:128, :] = part[1]

        def keep0(h, parts):
            h0s[net] = h
            keep_parts(x0, parts)

        def keep1(values, parts):
            for k, value in enumerate(values):
                a1[net, k] = value
            keep_parts(x1, parts)

        def keep2(values):
            for k, value in enumerate(values):
                a2[net, k] = value

        res[0:1, :] = res[0:1, :] + forward(get, xp[...], alpha[net], mm, keep0, keep1, keep2)

    def sides(value, low=0):
        return value[:, low : low + 64] + value[:, low + 64 : low + 128]

    def both(part):
        return jnp.concatenate(part, 0)

    def backward_wide(net, extra):
        get, mm = wide_tools(net)
        g2, g1, g0, dlast, dbias1, dbias0 = backward(
            get,
            alpha[net],
            res[1:2, :],
            mm,
            row_sums,
            h0s[net],
            [a1[net, k] for k in range(6)],
            [a2[net, k] for k in range(7)],
        )
        dm2 = dot_nt(
            jnp.concatenate([both(g) for g in g2], 1),
            jnp.concatenate([x1[net, k] for k in range(5)], 1),
        )
        ah = dot_nt(both(g1[0]), x0[net, 0])
        af = dot_nt(jnp.concatenate([both(g) for g in g1[1:4]], 0), x0[net, 1])
        al = dot_nt(both(g1[4]), x0[net, 2])
        pts = fold(dot_nt(both(g0), xpb[...]))
        af = [sides(fold(af[128 * d : 128 * (d + 1)])) for d in range(3)]
        scale, shift = affine(net)
        dm2, ah, al = [sides(fold(value)) for value in (dm2, ah, al)]
        finish(net, scale, shift, dm2, ah, af, al, pts, dlast, dbias1, dbias0, extra)

    half = lax.broadcasted_iota(jnp.int32, (1, pair), 1) < slots
    first_half = jnp.where(lower, 1.0, 0.0).astype(bf16)
    second_half = jnp.where(lower, 0.0, 1.0).astype(bf16)

    def face_get(k):
        return fcols[k]

    def face_mm(ref, low, high, streams):
        rows = high - low
        number = len(streams)
        mask = (lax.broadcasted_iota(jnp.int32, (1, number * pair), 1) & (pair - 1)) < slots
        pieces = []
        for axis in range(3):
            net = 3 + 2 * axis
            span = slice(axis * pair, (axis + 1) * pair)
            lhs = jnp.concatenate([ref[net, low:high, :], ref[net + 1, low:high, :]], 0)
            out = dot(lhs, jnp.concatenate([stream[:, span] for stream in streams], 1))
            out = jnp.where(mask, out[0:rows], out[rows : 2 * rows])
            pieces.append([out[:, pair * k : pair * (k + 1)] for k in range(number)])
        return [jnp.concatenate([piece[k] for piece in pieces], 1) for k in range(number)]

    def half_sums(value):
        return [
            row_sums(jnp.where(half if face % 2 == 0 else ~half, value[:, pair * (face // 2) : pair * (face // 2 + 1)], 0.0))
            for face in range(6)
        ]

    def forward_faces():
        def keep_parts(ref, parts):
            for k, part in enumerate(parts):
                ref[k, 0:64, :] = part[0] * first_half
                ref[k, 64:128, :] = part[1] * first_half
                ref[k, 128:192, :] = part[0] * second_half
                ref[k, 192:256, :] = part[1] * second_half

        def keep0(h, parts):
            fh0s[...] = h
            keep_parts(fx0, parts)

        def keep1(values, parts):
            for k, value in enumerate(values):
                fa1[k] = value
            keep_parts(fx1, parts)

        def keep2(values):
            for k, value in enumerate(values):
                fa2[k] = value

        row = forward(face_get, xf[...], falpha[...], face_mm, keep0, keep1, keep2)
        terms = jnp.concatenate([term.astype(f32) for term in three(row)] + [jnp.zeros((5, near), f32)], 0)
        spread = dot_nt(terms.astype(bf16), hot[...])
        res[0:1, :] = res[0:1, :] + (spread[0:1] + spread[1:2] + spread[2:3])

    def backward_faces():
        g2, g1, g0, dlast, dbias1, dbias0 = backward(
            face_get,
            falpha[...],
            fdelta[0:1, :],
            face_mm,
            half_sums,
            fh0s[...],
            [fa1[k] for k in range(6)],
            [fa2[k] for k in range(7)],
        )
        for axis in range(3):
            span = slice(axis * pair, (axis + 1) * pair)

            def cut(part):
                return jnp.concatenate([part[0][:, span], part[1][:, span]], 0)

            dm2 = fold(
                dot_nt(
                    jnp.concatenate([cut(g) for g in g2], 1),
                    jnp.concatenate([fx1[k, :, span] for k in range(5)], 1),
                )
            )
            ah = fold(dot_nt(cut(g1[0]), fx0[0, :, span]))
            af = dot_nt(jnp.concatenate([cut(g) for g in g1[1:4]], 0), fx0[1, :, span])
            af = [fold(af[128 * d : 128 * (d + 1)]) for d in range(3)]
            al = fold(dot_nt(cut(g1[4]), fx0[2, :, span]))
            for side in range(2):
                face = 2 * axis + side
                kept = (first_half if side == 0 else second_half)[:, span]
                pts = fold(dot_nt(cut(g0), xfb[:, span] * kept))
                scale, shift = face_affine(face)
                finish(
                    3 + face,
                    scale,
                    shift,
                    sides(dm2, 128 * side),
                    sides(ah, 128 * side),
                    [sides(v, 128 * side) for v in af],
                    sides(al, 128 * side),
                    pts,
                    dlast[face],
                    dbias1[face],
                    dbias0[face],
                    jnp.zeros((1, 64), f32),
                )

    def total(ref, number):
        value = ref[0]
        for k in range(1, number):
            value = value + ref[k]
        return value

    def tile_copy(tile):
        return pltpu.make_async_remote_copy(
            src_ref=grads.at[0, 8 * tile : 8 * tile + 8, :],
            dst_ref=tiles.at[here],
            send_sem=tile_send.at[tile],
            recv_sem=tile_recv.at[here],
            device_id=(tile * stride // sizes[1], tile * stride % sizes[1], me[2]),
            device_id_type=MESH,
        )

    def tile_arrival(sender):
        return pltpu.make_async_remote_copy(
            src_ref=grads.at[0, 0:8, :],
            dst_ref=tiles.at[sender],
            send_sem=tile_send.at[0],
            recv_sem=tile_recv.at[sender],
            device_id=in_plane(sender),
            device_id_type=MESH,
        )

    def along_z(source_ref, ref, send, recv, offset, sender):
        return pltpu.make_async_remote_copy(
            src_ref=source_ref,
            dst_ref=ref.at[sender],
            send_sem=send.at[offset],
            recv_sem=recv.at[sender],
            device_id=peer(2, offset),
            device_id_type=MESH,
        )

    def level_copy(offset, arriving):
        sender = lax.rem(me[2] + (sizes[2] - offset), sizes[2]) if arriving else me[2]
        return along_z(levels.at[me[2]], levels, level_send, level_recv, offset, sender)

    def column_copy(offset, arriving):
        sender = lax.rem(me[2] + (sizes[2] - offset), sizes[2]) if arriving else me[2]
        return along_z(grads.at[1], columns, column_send, column_recv, offset, sender)

    def share_copy(offset):
        return pltpu.make_async_remote_copy(
            src_ref=summed.at[my_rows, :],
            dst_ref=summed.at[my_rows, :],
            send_sem=share_send.at[offset],
            recv_sem=share_recv.at[lax.rem(here // stride, TILES)],
            device_id=in_plane(lax.rem(here + offset, plane)),
            device_id_type=MESH,
        )

    def share_arrival(tile):
        rows = summed.at[8 * tile : 8 * tile + 8, :]
        return pltpu.make_async_remote_copy(
            src_ref=rows,
            dst_ref=rows,
            send_sem=share_send.at[0],
            recv_sem=share_recv.at[tile],
            device_id=in_plane(tile * stride),
            device_id_type=MESH,
        )

    def send_back(face):
        axis, up = face // 2, face % 2
        return pltpu.make_async_remote_copy(
            src_ref=grads.at[3 + face],
            dst_ref=back.at[face ^ 1],
            send_sem=back_send.at[face],
            recv_sem=back_recv.at[face ^ 1],
            device_id=peer(axis, 2 * up - 1),
            device_id_type=MESH,
        )

    def give(value, first_ref, mid_ref, last_ref):
        mid_ref[0] = value[0:64, 0:64]
        mid_ref[1] = value[0:64, 64:128]
        first_ref[...] = value[64:68, 0:64]
        for k in range(3):
            if len(last_ref.shape) == 3:
                last_ref[k] = value[68 + k : 69 + k, 0:64]
            else:
                last_ref[k : k + 1, :] = value[68 + k : 69 + k, 0:64]

    res[0:1, :] = -source[...]

    def wide(net, carry):
        prepare_forward(net, *affine(net))
        forward_wide(net)
        return carry

    lax.fori_loop(0, 3, wide, 0)
    prepare_backward(0)
    for face in faces:
        halo(face).wait()
    for face in range(6):
        prepare_forward(3 + face, *face_affine(face))
    for k in range(7):
        fcols[k] = jnp.concatenate(
            [
                jnp.where(half, cols[3 + 2 * axis, :, k : k + 1], cols[4 + 2 * axis, :, k : k + 1])
                for axis in range(3)
            ],
            1,
        )
    forward_faces()

    residual = res[0:1, :]
    residual_out[...] = residual
    delta = residual * (1.0 / count)
    res[1:2, :] = delta
    loss = jnp.sum(residual * residual, axis=1, keepdims=True) * (0.5 / count)

    first_lane = lax.broadcasted_iota(jnp.int32, (1, 64), 1) == 0
    backward_wide(0, jnp.where(first_lane, loss, 0.0))
    for tile in range(TILES):
        pl.when(here != tile * stride)(tile_copy(tile).start)

    prepare_backward(1)
    backward_wide(1, jnp.zeros((1, 64), f32))
    columns[me[2]] = grads[1]
    for offset in range(1, sizes[2]):
        column_copy(offset, False).start()

    terms = jnp.concatenate([term.astype(f32) for term in three(delta)] + [jnp.zeros((5, count), f32)], 0)
    taken = dot(terms.astype(bf16), hot[...])
    fdelta[0:1, :] = taken[0:1] + taken[1:2] + taken[2:3]

    def prepare_rest(net, carry):
        prepare_backward(net)
        return carry

    lax.fori_loop(2, 9, prepare_rest, 0)
    backward_faces()
    for face in faces:
        send_back(face).start()

    @pl.when(reducer)
    def _():
        tiles[here] = grads[0, my_rows, :]
        for offset in range(1, plane):
            tile_arrival(lax.rem(here + offset, plane)).wait_recv()
        levels[me[2]] = total(tiles, plane)
        for offset in range(1, sizes[2]):
            level_copy(offset, False).start()

    backward_wide(2, jnp.zeros((1, 64), f32))

    for face in faces:
        send_back(face).wait()
    give(grads[2] + total(back, 6), fine_first_out, fine_mid_out, fine_last_out)
    for offset in range(1, sizes[2]):
        column_copy(offset, True).wait_recv()
    give(total(columns, sizes[2]), column_first_out, column_mid_out, column_last_out)

    @pl.when(reducer)
    def _():
        for offset in range(1, sizes[2]):
            level_copy(offset, True).wait_recv()
        summed[my_rows, :] = total(levels, sizes[2])
        for offset in range(1, plane):
            share_copy(offset).start()

    for offset in range(1, sizes[2]):
        column_copy(offset, False).wait_send()
    for tile in range(TILES):
        pl.when(here != tile * stride)(tile_copy(tile).wait_send)
    for tile in range(TILES):
        pl.when(here != tile * stride)(share_arrival(tile).wait_recv)
    value = summed[...]
    give(value, global_first_out, global_mid_out, global_last_out)
    loss_out[...] = value[71:72, 0:1]

    @pl.when(reducer)
    def _():
        for offset in range(1, sizes[2]):
            level_copy(offset, False).wait_send()
        for offset in range(1, plane):
            share_copy(offset).wait_send()


def hand_over(*refs):
    number = len(refs) // 2
    ins, outs, sem = refs[:number], refs[number : 2 * number], refs[2 * number]
    copies = [pltpu.make_async_copy(ins[k], outs[k], sem.at[k]) for k in range(number - 1)]
    for copy in copies:
        copy.start()
    outs[number - 1][...] = ins[number - 1][...]
    for copy in copies:
        copy.wait()


def step(sizes, points, band_index, source, *params):
    count = points.shape[-1]
    slots = band_index.shape[-1]
    near = 6 * slots
    plane = sizes[0] * sizes[1]
    operands = [points.reshape(3, 1, count), band_index.reshape(6, 1, slots), source.reshape(1, count)]
    shapes = [(4, 64), (2, 64, 64), (3, 1, 64)] * 2 + [(4, 64), (2, 64, 64), (3, 64)]
    operands += [param.reshape(shape) for param, shape in zip(params, shapes)]
    outs = [jax.ShapeDtypeStruct(shape, f32) for shape in [(1, count)] + shapes + [(1, 1)]]
    vmem = pltpu.VMEM
    scratch = [vmem(value.shape, value.dtype) for value in operands]
    scratch += [
        vmem((9, 72, 128), f32),
        vmem((9, 72, 128), f32),
        vmem((9, 320, 192), bf16),
        vmem((9, 64, 192), bf16),
        vmem((9, 64, 192), bf16),
        vmem((9, 64, 192), bf16),
        vmem((9, 64, 576), bf16),
        vmem((9, 64, 192), bf16),
        vmem((9, 64, 128), f32),
        vmem((8, count), f32),
        vmem((128, count), bf16),
        vmem((3, 8, count), f32),
        vmem((3, 3, 128, count), bf16),
        vmem((3, 5, 128, count), bf16),
        vmem((3, 64, count), f32),
        vmem((3, 6, 64, count), f32),
        vmem((3, 7, 64, count), f32),
        vmem((8, count), f32),
        vmem((8, near), f32),
        vmem((128, near), bf16),
        vmem((8, near), f32),
        vmem((7, 64, near), f32),
        vmem((3, 256, near), bf16),
        vmem((5, 256, near), bf16),
        vmem((64, near), f32),
        vmem((6, 64, near), f32),
        vmem((7, 64, near), f32),
        vmem((8, near), f32),
        vmem((count, near), bf16),
        vmem((6, 72, 128), f32),
        vmem((plane, 8, 128), f32),
        vmem((sizes[2], 8, 128), f32),
        vmem((72, 128), f32),
        vmem((sizes[2], 72, 128), f32),
    ]
    dma = pltpu.SemaphoreType.DMA
    scratch += [dma((12,))] + [dma((6,))] * 4
    scratch += [dma((number,)) for number in (TILES, plane, sizes[2], sizes[2], plane, TILES, sizes[2], sizes[2])]
    whole = pl.BlockSpec(memory_space=pltpu.VMEM)
    outside = pl.BlockSpec(memory_space=pltpu.HBM)
    results = pl.pallas_call(
        functools.partial(kernel, sizes),
        out_shape=[vmem(value.shape, value.dtype) for value in outs],
        in_specs=[outside] * 12,
        out_specs=[whole] * 11,
        scratch_shapes=scratch,
        compiler_params=pltpu.CompilerParams(
            collective_id=0, has_side_effects=True, vmem_limit_bytes=32 << 20
        ),
        cost_estimate=pl.CostEstimate(flops=500_000_000, bytes_accessed=1_000_000, transcendentals=400_000),
        name="training_step",
    )(*[pltpu.with_memory_space_constraint(value, pltpu.HBM) for value in operands])
    results = pl.pallas_call(
        hand_over,
        out_shape=outs,
        in_specs=[whole] * 11,
        out_specs=[outside] * 10 + [whole],
        scratch_shapes=[dma((10,))],
        compiler_params=pltpu.CompilerParams(vmem_limit_bytes=1 << 20),
        cost_estimate=pl.CostEstimate(flops=0, bytes_accessed=400_000, transcendentals=0),
        name="hand_over",
    )(*results)
    ranks = [params[k].shape for k in range(9)]
    arrays = [results[0].reshape(source.shape)]
    arrays += [value.reshape(shape) for value, shape in zip(results[1:10], ranks)]
    return tuple(arrays) + (results[10].reshape(()),)


def solution(mesh):
    sizes = tuple(mesh.shape[axis] for axis in AXES)
    cell = ("gx", "gy", "gz")
    column = ("gx", "gy")
    in_specs = (P(*cell, None, None), P(*cell, None, None), P(*cell, None))
    nets_specs = (
        (P(*cell, None, None), P(*cell, None, None, None), P(*cell, None, None))
        + (P(*column, None, None), P(*column, None, None, None), P(*column, None, None))
        + (P(), P(), P())
    )
    return jax.shard_map(
        functools.partial(step, sizes),
        mesh=mesh,
        in_specs=in_specs + nets_specs,
        out_specs=(P(*cell, None),) + nets_specs + (P(),),
        check_vma=False,
    )
```

```python
import functools

import jax
import jax.numpy as jnp
from jax import lax
from jax.experimental import pallas as pl
from jax.experimental.pallas import tpu as pltpu
from jax.sharding import PartitionSpec as P

MESH = pl.DeviceIdType.MESH
AXES = ("gx", "gy", "gz")
f32, bf16 = jnp.float32, jnp.bfloat16
wave_square = 4.0
inverse_depth = 8.0
TILES = 9
NT = (((1,), (1,)), ((), ()))


def split(value):
    high = value.astype(bf16)
    return high, (value - high.astype(f32)).astype(bf16)


def three(value):
    first = value.astype(bf16)
    rest = value - first.astype(f32)
    second = rest.astype(bf16)
    return first, second, (rest - second.astype(f32)).astype(bf16)


def left(matrix):
    high = matrix.astype(bf16).astype(f32)
    return jnp.concatenate([high, high, matrix - high], 1).astype(bf16)


def right(high, low):
    return jnp.concatenate([high, low, high], 0)


def dot(a, b):
    return jnp.dot(a, b, preferred_element_type=f32)


def dot_nt(a, b):
    return lax.dot_general(a, b, NT, preferred_element_type=f32)


def window(depth, facing):
    square = depth * depth
    smooth = depth * (15.0 - 10.0 * square + 3.0 * square * square) / 8.0
    blend = 0.5 * (1.0 - smooth)
    slope = (0.5 * inverse_depth * 15.0 / 8.0) * facing * (1.0 - square) * (1.0 - square)
    bend = (0.5 * inverse_depth * inverse_depth * 7.5) * depth * (1.0 - square)
    return blend, slope, bend


def tile_owners(sizes):
    chips = (sizes[1] + 1) // 2

    def order(place):
        x, chip = place // sizes[1], place % sizes[1] // 2
        return (x + chip + place) % 2, max(min(x, sizes[0] - x), min(chip, chips - chip)), place

    return sorted(range(sizes[0] * sizes[1]), key=order)[:TILES]


def far_first(sizes):
    def distance(offset):
        x, y = offset
        return -min(x, sizes[0] - x) - min(y, sizes[1] - y) / 2, x, y

    offsets = [(x, y) for x in range(sizes[0]) for y in range(sizes[1]) if x or y]
    return sorted(offsets, key=distance)


def kernel(sizes, *refs):
    (
        points_hbm,
        band_hbm,
        source_hbm,
        fine_first_hbm,
        fine_mid_hbm,
        fine_last_hbm,
        column_first_hbm,
        column_mid_hbm,
        column_last_hbm,
        global_first_hbm,
        global_mid_hbm,
        global_last_hbm,
        residual_out,
        fine_first_out,
        fine_mid_out,
        fine_last_out,
        column_first_out,
        column_mid_out,
        column_last_out,
        global_first_out,
        global_mid_out,
        global_last_out,
        loss_out,
        points,
        band,
        source,
        fine_first,
        fine_mid,
        fine_last,
        column_first,
        column_mid,
        column_last,
        global_first,
        global_mid,
        global_last,
        nets,
        grads,
        f1,
        f2,
        b2,
        b1h,
        b1s,
        b1p,
        cols,
        xp,
        xpb,
        alpha,
        x0,
        x1,
        h0s,
        a1,
        a2,
        res,
        xf,
        xfb,
        falpha,
        fcols,
        fx0,
        fx1,
        fh0s,
        fa1,
        fa2,
        fdelta,
        hot,
        back,
        tiles,
        levels,
        summed,
        columns,
        column_sum,
        load_sem,
        halo_send,
        halo_recv,
        back_send,
        back_recv,
        tile_send,
        tile_recv,
        level_send,
        level_recv,
        share_send,
        share_recv,
        column_send,
        column_recv,
        gather_send,
        gather_recv,
    ) = refs
    me = tuple(lax.axis_index(axis) for axis in AXES)
    count = points.shape[2]
    slots = band.shape[2]
    pair = 2 * slots
    near = 6 * slots
    plane = sizes[0] * sizes[1]
    here = me[0] * sizes[1] + me[1]
    owners = tile_owners(sizes)
    reducer = here == owners[0]
    my_tile = jnp.int32(0)
    for tile in range(1, TILES):
        reducer = reducer | (here == owners[tile])
        my_tile = jnp.where(here == owners[tile], tile, my_tile)
    my_rows = pl.ds(pl.multiple_of(8 * my_tile, 8), 8)

    def peer(axis, offset):
        other = list(me)
        other[axis] = lax.rem(me[axis] + (offset + sizes[axis]), sizes[axis])
        return tuple(other)

    def in_plane(place):
        return (place // sizes[1], lax.rem(place, sizes[1]), me[2])

    barrier = pltpu.get_barrier_semaphore()
    friends = [in_plane(lax.rem(here + offset, plane)) for offset in range(1, plane)]
    friends += [peer(2, offset) for offset in range(1, sizes[2])]
    for friend in friends:
        pl.semaphore_signal(barrier, inc=1, device_id=friend, device_id_type=MESH)

    loads = [
        pltpu.make_async_copy(refs[k], refs[23 + k], load_sem.at[k])
        for k in (4, 3, 5, 0, 1, 2, 10, 9, 11, 7, 6, 8)
    ]
    for load in loads:
        load.start()

    def pack(net, first, mid, last):
        nets[net, 0:64, :] = jnp.concatenate([mid[0], mid[1]], 1)
        nets[net, 64:68, 0:64] = first[...]
        for k in range(3):
            nets[net, 68 + k : 69 + k, 0:64] = last[k] if len(last.shape) == 3 else last[k : k + 1, :]
        nets[net, 71:72, 0:64] = jnp.zeros((1, 64), f32)
        nets[net, 64:72, 64:128] = jnp.zeros((8, 64), f32)

    for load in loads[:3]:
        load.wait()
    pack(2, fine_first, fine_mid, fine_last)
    for load in loads[3:]:
        load.wait()
    pack(1, column_first, column_mid, column_last)
    pack(0, global_first, global_mid, global_last)

    def halo(face):
        axis, up = face // 2, face % 2
        return pltpu.make_async_remote_copy(
            src_ref=nets.at[2],
            dst_ref=nets.at[3 + (face ^ 1)],
            send_sem=halo_send.at[face],
            recv_sem=halo_recv.at[face ^ 1],
            device_id=peer(axis, 2 * up - 1),
            device_id_type=MESH,
        )

    faces = [face for face in range(6) if sizes[face // 2] > 1]
    place = [me[axis].astype(f32) for axis in range(3)]

    def affine(net):
        scale, shift = [], []
        for axis in range(3):
            fitted_scale = 2.0 / sizes[axis]
            fitted_shift = (2.0 * place[axis] + 1.0) * (1.0 / sizes[axis]) - 1.0
            fitted = (net == 0) if axis < 2 else (net <= 1)
            scale.append(jnp.where(fitted, fitted_scale, 2.0))
            shift.append(jnp.where(fitted, fitted_shift, 0.0))
        return scale, shift

    def face_affine(face):
        shift = [0.0, 0.0, 0.0]
        shift[face // 2] = 2.0 - 4.0 * (face % 2)
        return [2.0, 2.0, 2.0], shift

    def prepare_forward(net, scale, shift):
        mats = nets[net, 0:64, :]
        rows = nets[net, 64:72, :]
        turned = rows.T
        m1 = mats[:, 0:64]
        row = [scale[d] * rows[d : d + 1, 0:64] for d in range(3)]
        square = -2.0 * (row[0] * row[0] + row[1] * row[1] + row[2] * row[2])
        bias = turned[0:64, 3:4]
        for d in range(3):
            bias = bias + shift[d] * turned[0:64, d : d + 1]
        f1[net, 0:64, :] = left(m1)
        for d in range(3):
            f1[net, 64 * (d + 1) : 64 * (d + 2), :] = left(m1 * row[d])
        f1[net, 256:320, :] = left(m1 * square)
        f2[net] = left(mats[:, 64:128])
        lane = lax.broadcasted_iota(jnp.int32, (64, 8), 1)
        kept = turned[0:64, 0:8]
        for d in range(3):
            kept = jnp.where(lane == d, scale[d] * kept, kept)
        cols[net, :, 0:8] = jnp.where(lane == 3, bias, kept)

    def prepare_backward(net):
        turned = nets[net, 0:64, :].T
        m1t = turned[0:64]
        b1h[net] = left(m1t)
        col = [cols[net, :, d : d + 1] for d in range(3)]
        scaled = [m1t * col[d] for d in range(3)]
        high = [value.astype(bf16).astype(f32) for value in scaled]
        low = [scaled[d] - high[d] for d in range(3)]
        b1s[net] = jnp.concatenate(high + high + low, 1).astype(bf16)
        b1p[net] = left(m1t * (-2.0 * (col[0] * col[0] + col[1] * col[1] + col[2] * col[2])))
        b2[net] = left(turned[64:128])

    lane_ones = jnp.ones((1, count), f32)
    for d in range(3):
        xp[d : d + 1, :] = points[d]
    xp[3:4, :] = lane_ones
    xp[4:8, :] = jnp.zeros((4, count), f32)
    x_terms = three(xp[...])
    xpb[...] = jnp.zeros(xpb.shape, bf16)
    xpb[0:16, :] = jnp.concatenate([x_terms[0].astype(f32), x_terms[1].astype(f32)], 0).astype(bf16)

    def present(face):
        axis = face // 2
        there = me[axis] < sizes[axis] - 1 if face % 2 else me[axis] > 0
        return jnp.where(there, 1.0, 0.0).astype(f32)

    inside = lane_ones
    curve = jnp.zeros((1, count), f32)
    for axis in range(3):
        along = points[axis]
        upper = along > 0.0
        facing = jnp.where(upper, 1.0, -1.0)
        depth = jnp.minimum((0.5 - jnp.abs(along)) * inverse_depth, 1.0)
        exists = jnp.where(upper, present(2 * axis + 1), present(2 * axis))
        blend, slope, bend = window(depth, facing)
        inside = inside - exists * blend
        curve = curve - exists * bend
        alpha[2, 1 + axis : 2 + axis, :] = -2.0 * exists * slope
    alpha[2, 0:1, :] = wave_square * inside + curve
    alpha[2, 4:5, :] = inside
    for net in (0, 1):
        alpha[net, 0:1, :] = wave_square * lane_ones
        alpha[net, 1:4, :] = jnp.zeros((3, count), f32)
        alpha[net, 4:5, :] = lane_ones

    if friends:
        pl.semaphore_wait(barrier, len(friends))
    for face in faces:
        halo(face).start()

    near_lane = lax.broadcasted_iota(jnp.int32, (1, near), 1)
    face_of = near_lane // slots
    lower = lax.rem(face_of, 2) == 0
    stacked = jnp.concatenate([term.astype(f32) for term in x_terms], 0).astype(bf16)
    point_id = lax.broadcasted_iota(jnp.int32, (count, near), 0)
    listed = jnp.concatenate([band[face] for face in range(6)], 1)
    hot[...] = jnp.where(point_id == listed, 1.0, 0.0).astype(bf16)
    taken = dot(stacked, hot[...])
    taken = taken[0:8] + taken[8:16] + taken[16:24]
    xf[...] = taken
    high, low = split(taken)
    xfb[...] = jnp.zeros(xfb.shape, bf16)
    xfb[0:16, :] = jnp.concatenate([high.astype(f32), low.astype(f32)], 0).astype(bf16)
    facing = jnp.where(lower, -1.0, 1.0)
    axis_of = face_of // 2
    along = jnp.where(axis_of == 0, taken[0:1], jnp.where(axis_of == 1, taken[1:2], taken[2:3]))
    exists = jnp.zeros((1, near), f32)
    for face in range(6):
        exists = jnp.where(face_of == face, present(face), exists)
    depth = jnp.minimum((0.5 - facing * along) * inverse_depth, 1.0)
    blend, slope, bend = window(depth, facing)
    falpha[0:1, :] = exists * (wave_square * blend + bend)
    for d in range(3):
        falpha[1 + d : 2 + d, :] = jnp.where(axis_of == d, 2.0 * exists * slope, 0.0)
    falpha[4:5, :] = exists * blend

    def tanh_layer(z, f, m):
        h = jnp.tanh(z)
        s = 1.0 - h * h
        q = f[0] * f[0] + f[1] * f[1] + f[2] * f[2]
        return h, s, q, m - 2.0 * h * q

    def forward(get, x, al, mm, keep0, keep1, keep2):
        z = get(0) * x[0:1] + get(1) * x[1:2] + get(2) * x[2:3] + get(3)
        h = jnp.tanh(z)
        s = 1.0 - h * h
        p = h * s
        parts = [split(v) for v in (h, s, p)]
        keep0(h, parts)
        m1h = mm(f1, 0, 64, [right(*parts[0])])[0]
        m1f = mm(f1, 64, 256, [right(*parts[1])])[0]
        m1l = mm(f1, 256, 320, [right(*parts[2])])[0]
        f = [m1f[64 * d : 64 * (d + 1)] for d in range(3)]
        h, s, q, w = tanh_layer(m1h + get(4), f, m1l)
        parts = [split(v) for v in (h, s * f[0], s * f[1], s * f[2], s * w)]
        keep1((h, f[0], f[1], f[2], q, w), parts)
        out = mm(f2, 0, 64, [right(*part) for part in parts])
        f = out[1:4]
        h, s, q, w = tanh_layer(out[0] + get(5), f, out[4])
        u = al[1:2] * f[0] + al[2:3] * f[1] + al[3:4] * f[2] + al[4:5] * w
        c = al[0:1] * h + s * u
        keep2((h, f[0], f[1], f[2], q, u, c))
        return jnp.sum(get(6) * c, axis=0, keepdims=True)

    def backward(get, al, delta, mm, lane_sum, saved0, saved1, saved2):
        h, fa, fb, fc, q, u, c = saved2
        f = (fa, fb, fc)
        dlast = lane_sum(delta * c)
        e = get(6) * delta
        s = 1.0 - h * h
        es = e * s
        gm = es * al[4:5]
        k = 4.0 * h * gm
        gf = [es * al[1 + d : 2 + d] - k * f[d] for d in range(3)]
        gz = (e * al[0:1] - 2.0 * (q * gm + h * (e * u))) * s
        dbias1 = lane_sum(gz)
        g2 = [split(v) for v in (gz, gf[0], gf[1], gf[2], gm)]
        oh, oa, ob, oc, ol = mm(b2, 0, 64, [right(*part) for part in g2])
        o = (oa, ob, oc)
        h, fa, fb, fc, q, w = saved1
        f = (fa, fb, fc)
        s = 1.0 - h * h
        gm = ol * s
        k = 4.0 * h * gm
        gf = [o[d] * s - k * f[d] for d in range(3)]
        gs = o[0] * f[0] + o[1] * f[1] + o[2] * f[2] + ol * w
        gz = (oh - 2.0 * (q * gm + h * gs)) * s
        dbias0 = lane_sum(gz)
        g1 = [split(v) for v in (gz, gf[0], gf[1], gf[2], gm)]
        oh = mm(b1h, 0, 64, [right(*g1[0])])[0]
        os = mm(b1s, 0, 64, [jnp.concatenate([g1[d][k] for k in (0, 1, 0) for d in (1, 2, 3)], 0)])[0]
        op = mm(b1p, 0, 64, [right(*g1[4])])[0]
        h = saved0
        s = 1.0 - h * h
        gz = (oh + op * s - 2.0 * h * (os + op * h)) * s
        return g2, g1, split(gz), dlast, dbias1, dbias0

    def fold(product):
        return product[0:64] + product[64:128]

    def finish(net, scale, shift, dm2, ah, af, al, pts, dlast, dbias1, dbias0, extra):
        lane = lax.broadcasted_iota(jnp.int32, (64, 128), 1)
        pts = jnp.where(lane == 4, dbias0, pts)
        pts = jnp.where(lane == 5, dbias1, pts)
        pts = jnp.where(lane == 6, dlast, pts)
        turned = pts.T
        sums = turned[0:8] + turned[8:16]
        m1 = nets[net, 0:64, 0:64]
        rows = nets[net, 64:72, 0:64]
        row = [scale[d] * rows[d : d + 1] for d in range(3)]
        square = row[0] * row[0] + row[1] * row[1] + row[2] * row[2]
        dsquare = -2.0 * jnp.sum(m1 * al, axis=0, keepdims=True)
        dm1 = ah - 2.0 * (al * square)
        first = []
        for d in range(3):
            dm1 = dm1 + af[d] * row[d]
            slope = sums[d : d + 1] + jnp.sum(m1 * af[d], axis=0, keepdims=True) + 2.0 * row[d] * dsquare
            first.append(scale[d] * slope + shift[d] * sums[3:4])
        grads[net, 0:64, :] = jnp.concatenate([dm1, dm2], 1)
        grads[net, 64:72, 0:64] = jnp.concatenate(first + [sums[3:7], extra], 0)
        grads[net, 64:72, 64:128] = jnp.zeros((8, 64), f32)

    def wide_tools(net):
        def get(k):
            return cols[net, :, k : k + 1]

        def mm(ref, low, high, streams):
            out = dot(ref[net, low:high, :], jnp.concatenate(streams, 1))
            return [out[:, count * k : count * (k + 1)] for k in range(len(streams))]

        return get, mm

    def row_sums(value):
        return jnp.sum(value, axis=1, keepdims=True)

    def forward_wide(net):
        get, mm = wide_tools(net)

        def keep_parts(ref, parts):
            for k, part in enumerate(parts):
                ref[net, k, 0:64, :] = part[0]
                ref[net, k, 64:128, :] = part[1]

        def keep0(h, parts):
            h0s[net] = h
            keep_parts(x0, parts)

        def keep1(values, parts):
            for k, value in enumerate(values):
                a1[net, k] = value
            keep_parts(x1, parts)

        def keep2(values):
            for k, value in enumerate(values):
                a2[net, k] = value

        res[0:1, :] = res[0:1, :] + forward(get, xp[...], alpha[net], mm, keep0, keep1, keep2)

    def sides(value, low=0):
        return value[:, low : low + 64] + value[:, low + 64 : low + 128]

    def both(part):
        return jnp.concatenate(part, 0)

    def backward_wide(net, extra):
        get, mm = wide_tools(net)
        g2, g1, g0, dlast, dbias1, dbias0 = backward(
            get,
            alpha[net],
            res[1:2, :],
            mm,
            row_sums,
            h0s[net],
            [a1[net, k] for k in range(6)],
            [a2[net, k] for k in range(7)],
        )
        dm2 = dot_nt(
            jnp.concatenate([both(g) for g in g2], 1),
            jnp.concatenate([x1[net, k] for k in range(5)], 1),
        )
        ah = dot_nt(both(g1[0]), x0[net, 0])
        af = dot_nt(jnp.concatenate([both(g) for g in g1[1:4]], 0), x0[net, 1])
        al = dot_nt(both(g1[4]), x0[net, 2])
        pts = fold(dot_nt(both(g0), xpb[...]))
        af = [sides(fold(af[128 * d : 128 * (d + 1)])) for d in range(3)]
        scale, shift = affine(net)
        dm2, ah, al = [sides(fold(value)) for value in (dm2, ah, al)]
        finish(net, scale, shift, dm2, ah, af, al, pts, dlast, dbias1, dbias0, extra)

    half = lax.broadcasted_iota(jnp.int32, (1, pair), 1) < slots
    first_half = jnp.where(lower, 1.0, 0.0).astype(bf16)
    second_half = jnp.where(lower, 0.0, 1.0).astype(bf16)

    def face_get(k):
        return fcols[k]

    def face_mm(ref, low, high, streams):
        rows = high - low
        number = len(streams)
        mask = (lax.broadcasted_iota(jnp.int32, (1, number * pair), 1) & (pair - 1)) < slots
        pieces = []
        for axis in range(3):
            net = 3 + 2 * axis
            span = slice(axis * pair, (axis + 1) * pair)
            lhs = jnp.concatenate([ref[net, low:high, :], ref[net + 1, low:high, :]], 0)
            out = dot(lhs, jnp.concatenate([stream[:, span] for stream in streams], 1))
            out = jnp.where(mask, out[0:rows], out[rows : 2 * rows])
            pieces.append([out[:, pair * k : pair * (k + 1)] for k in range(number)])
        return [jnp.concatenate([piece[k] for piece in pieces], 1) for k in range(number)]

    def half_sums(value):
        return [
            row_sums(jnp.where(half if face % 2 == 0 else ~half, value[:, pair * (face // 2) : pair * (face // 2 + 1)], 0.0))
            for face in range(6)
        ]

    def forward_faces():
        def keep_parts(ref, parts):
            for k, part in enumerate(parts):
                ref[k, 0:64, :] = part[0] * first_half
                ref[k, 64:128, :] = part[1] * first_half
                ref[k, 128:192, :] = part[0] * second_half
                ref[k, 192:256, :] = part[1] * second_half

        def keep0(h, parts):
            fh0s[...] = h
            keep_parts(fx0, parts)

        def keep1(values, parts):
            for k, value in enumerate(values):
                fa1[k] = value
            keep_parts(fx1, parts)

        def keep2(values):
            for k, value in enumerate(values):
                fa2[k] = value

        row = forward(face_get, xf[...], falpha[...], face_mm, keep0, keep1, keep2)
        terms = jnp.concatenate([term.astype(f32) for term in three(row)] + [jnp.zeros((5, near), f32)], 0)
        spread = dot_nt(terms.astype(bf16), hot[...])
        res[0:1, :] = res[0:1, :] + (spread[0:1] + spread[1:2] + spread[2:3])

    def backward_faces():
        g2, g1, g0, dlast, dbias1, dbias0 = backward(
            face_get,
            falpha[...],
            fdelta[0:1, :],
            face_mm,
            half_sums,
            fh0s[...],
            [fa1[k] for k in range(6)],
            [fa2[k] for k in range(7)],
        )
        for axis in range(3):
            span = slice(axis * pair, (axis + 1) * pair)

            def cut(part):
                return jnp.concatenate([part[0][:, span], part[1][:, span]], 0)

            dm2 = fold(
                dot_nt(
                    jnp.concatenate([cut(g) for g in g2], 1),
                    jnp.concatenate([fx1[k, :, span] for k in range(5)], 1),
                )
            )
            ah = fold(dot_nt(cut(g1[0]), fx0[0, :, span]))
            af = dot_nt(jnp.concatenate([cut(g) for g in g1[1:4]], 0), fx0[1, :, span])
            af = [fold(af[128 * d : 128 * (d + 1)]) for d in range(3)]
            al = fold(dot_nt(cut(g1[4]), fx0[2, :, span]))
            for side in range(2):
                face = 2 * axis + side
                kept = (first_half if side == 0 else second_half)[:, span]
                pts = fold(dot_nt(cut(g0), xfb[:, span] * kept))
                scale, shift = face_affine(face)
                finish(
                    3 + face,
                    scale,
                    shift,
                    sides(dm2, 128 * side),
                    sides(ah, 128 * side),
                    [sides(v, 128 * side) for v in af],
                    sides(al, 128 * side),
                    pts,
                    dlast[face],
                    dbias1[face],
                    dbias0[face],
                    jnp.zeros((1, 64), f32),
                )

    def total(ref, number):
        value = ref[0]
        for k in range(1, number):
            value = value + ref[k]
        return value

    def tile_copy(tile):
        return pltpu.make_async_remote_copy(
            src_ref=grads.at[0, 8 * tile : 8 * tile + 8, :],
            dst_ref=tiles.at[here],
            send_sem=tile_send.at[tile],
            recv_sem=tile_recv.at[here],
            device_id=(owners[tile] // sizes[1], owners[tile] % sizes[1], me[2]),
            device_id_type=MESH,
        )

    def tile_arrival(sender):
        return pltpu.make_async_remote_copy(
            src_ref=grads.at[0, 0:8, :],
            dst_ref=tiles.at[sender],
            send_sem=tile_send.at[0],
            recv_sem=tile_recv.at[sender],
            device_id=in_plane(sender),
            device_id_type=MESH,
        )

    def along_z(source_ref, ref, send, recv, offset, sender):
        return pltpu.make_async_remote_copy(
            src_ref=source_ref,
            dst_ref=ref.at[sender],
            send_sem=send.at[offset],
            recv_sem=recv.at[sender],
            device_id=peer(2, offset),
            device_id_type=MESH,
        )

    def level_copy(offset, arriving):
        sender = lax.rem(me[2] + (sizes[2] - offset), sizes[2]) if arriving else me[2]
        return along_z(levels.at[me[2]], levels, level_send, level_recv, offset, sender)

    layers = -(-TILES // sizes[2])

    def column_copies(offset, arriving):
        target = lax.rem(me[2] + offset, sizes[2])
        sender = lax.rem(me[2] + (sizes[2] - offset), sizes[2]) if arriving else me[2]
        for layer in range(layers):
            tile = layer * sizes[2] + (me[2] if arriving else target)
            rows = pl.ds(pl.multiple_of(8 * lax.rem(tile, TILES), 8), 8)
            yield tile < TILES, pltpu.make_async_remote_copy(
                src_ref=grads.at[1, rows, :],
                dst_ref=columns.at[layer, sender],
                send_sem=column_send.at[layer, offset],
                recv_sem=column_recv.at[layer, sender],
                device_id=peer(2, offset),
                device_id_type=MESH,
            )

    def gather_copies(offset, arriving):
        sender = lax.rem(me[2] + (sizes[2] - offset), sizes[2]) if arriving else me[2]
        for layer in range(layers):
            tile = layer * sizes[2] + sender
            rows = pl.ds(pl.multiple_of(8 * lax.rem(tile, TILES), 8), 8)
            yield tile < TILES, pltpu.make_async_remote_copy(
                src_ref=column_sum.at[rows, :],
                dst_ref=column_sum.at[rows, :],
                send_sem=gather_send.at[layer, offset],
                recv_sem=gather_recv.at[layer, sender],
                device_id=peer(2, offset),
                device_id_type=MESH,
            )

    def own_layers():
        for layer in range(layers):
            tile = layer * sizes[2] + me[2]
            yield layer, tile < TILES, pl.ds(pl.multiple_of(8 * lax.rem(tile, TILES), 8), 8)

    def every(copies, arriving, action):
        for offset in range(1, sizes[2]):
            for needed, copy in copies(offset, arriving):
                pl.when(needed)(getattr(copy, action))

    def share_copy(number):
        x, y = far_first(sizes)[number]
        target = (lax.rem(me[0] + x, sizes[0]), lax.rem(me[1] + y, sizes[1]), me[2])
        return pltpu.make_async_remote_copy(
            src_ref=summed.at[my_rows, :],
            dst_ref=summed.at[my_rows, :],
            send_sem=share_send.at[number],
            recv_sem=share_recv.at[my_tile],
            device_id=target,
            device_id_type=MESH,
        )

    def share_arrival(tile):
        rows = summed.at[8 * tile : 8 * tile + 8, :]
        return pltpu.make_async_remote_copy(
            src_ref=rows,
            dst_ref=rows,
            send_sem=share_send.at[0],
            recv_sem=share_recv.at[tile],
            device_id=in_plane(owners[tile]),
            device_id_type=MESH,
        )

    def send_back(face):
        axis, up = face // 2, face % 2
        return pltpu.make_async_remote_copy(
            src_ref=grads.at[3 + face],
            dst_ref=back.at[face ^ 1],
            send_sem=back_send.at[face],
            recv_sem=back_recv.at[face ^ 1],
            device_id=peer(axis, 2 * up - 1),
            device_id_type=MESH,
        )

    def give(value, first_ref, mid_ref, last_ref):
        mid_ref[0] = value[0:64, 0:64]
        mid_ref[1] = value[0:64, 64:128]
        first_ref[...] = value[64:68, 0:64]
        for k in range(3):
            if len(last_ref.shape) == 3:
                last_ref[k] = value[68 + k : 69 + k, 0:64]
            else:
                last_ref[k : k + 1, :] = value[68 + k : 69 + k, 0:64]

    res[0:1, :] = -source[...]

    for net in range(3):
        prepare_forward(net, *affine(net))
        forward_wide(net)
    prepare_backward(0)
    for face in faces:
        halo(face).wait()
    for face in range(6):
        prepare_forward(3 + face, *face_affine(face))
    for k in range(7):
        fcols[k] = jnp.concatenate(
            [
                jnp.where(half, cols[3 + 2 * axis, :, k : k + 1], cols[4 + 2 * axis, :, k : k + 1])
                for axis in range(3)
            ],
            1,
        )
    forward_faces()

    residual = res[0:1, :]
    residual_out[...] = residual
    delta = residual * (1.0 / count)
    res[1:2, :] = delta
    loss = jnp.sum(residual * residual, axis=1, keepdims=True) * (0.5 / count)

    first_lane = lax.broadcasted_iota(jnp.int32, (1, 64), 1) == 0
    backward_wide(0, jnp.where(first_lane, loss, 0.0))
    for tile in range(TILES):
        pl.when(here != owners[tile])(tile_copy(tile).start)

    prepare_backward(1)
    backward_wide(1, jnp.zeros((1, 64), f32))
    every(column_copies, False, "start")

    terms = jnp.concatenate([term.astype(f32) for term in three(delta)] + [jnp.zeros((5, count), f32)], 0)
    taken = dot(terms.astype(bf16), hot[...])
    fdelta[0:1, :] = taken[0:1] + taken[1:2] + taken[2:3]

    for face in range(6):
        prepare_backward(3 + face)
    backward_faces()
    for face in faces:
        send_back(face).start()

    @pl.when(reducer)
    def _():
        tiles[here] = grads[0, my_rows, :]
        for offset in range(1, plane):
            tile_arrival(lax.rem(here + offset, plane)).wait_recv()
        levels[me[2]] = total(tiles, plane)
        for offset in range(1, sizes[2]):
            level_copy(offset, False).start()

    prepare_backward(2)
    backward_wide(2, jnp.zeros((1, 64), f32))

    for layer, needed, rows in own_layers():

        @pl.when(needed)
        def _(layer=layer, rows=rows):
            columns[layer, me[2]] = grads[1, rows, :]

    every(column_copies, True, "wait_recv")
    for layer, needed, rows in own_layers():

        @pl.when(needed)
        def _(layer=layer, rows=rows):
            column_sum[rows, :] = total(columns.at[layer], sizes[2])

    every(gather_copies, False, "start")

    for face in faces:
        send_back(face).wait()
    give(grads[2] + total(back, 6), fine_first_out, fine_mid_out, fine_last_out)

    @pl.when(reducer)
    def _():
        for offset in range(1, sizes[2]):
            level_copy(offset, True).wait_recv()
        summed[my_rows, :] = total(levels, sizes[2])
        for number in range(plane - 1):
            share_copy(number).start()

    every(gather_copies, True, "wait_recv")
    give(column_sum[...], column_first_out, column_mid_out, column_last_out)
    every(column_copies, False, "wait_send")
    every(gather_copies, False, "wait_send")
    for tile in range(TILES):
        pl.when(here != owners[tile])(tile_copy(tile).wait_send)
    for tile in range(TILES):
        pl.when(here != owners[tile])(share_arrival(tile).wait_recv)
    value = summed[...]
    give(value, global_first_out, global_mid_out, global_last_out)
    loss_out[...] = value[71:72, 0:1]

    @pl.when(reducer)
    def _():
        for offset in range(1, sizes[2]):
            level_copy(offset, False).wait_send()
        for number in range(plane - 1):
            share_copy(number).wait_send()


def hand_over(*refs):
    number = len(refs) // 2
    ins, outs, sem = refs[:number], refs[number : 2 * number], refs[2 * number]
    copies = [pltpu.make_async_copy(ins[k], outs[k], sem.at[k]) for k in range(number - 1)]
    for copy in copies:
        copy.start()
    outs[number - 1][...] = ins[number - 1][...]
    for copy in copies:
        copy.wait()


def step(sizes, points, band_index, source, *params):
    count = points.shape[-1]
    slots = band_index.shape[-1]
    near = 6 * slots
    plane = sizes[0] * sizes[1]
    layers = -(-TILES // sizes[2])
    operands = [points.reshape(3, 1, count), band_index.reshape(6, 1, slots), source.reshape(1, count)]
    shapes = [(4, 64), (2, 64, 64), (3, 1, 64)] * 2 + [(4, 64), (2, 64, 64), (3, 64)]
    operands += [param.reshape(shape) for param, shape in zip(params, shapes)]
    outs = [jax.ShapeDtypeStruct(shape, f32) for shape in [(1, count)] + shapes + [(1, 1)]]
    vmem = pltpu.VMEM
    scratch = [vmem(value.shape, value.dtype) for value in operands]
    scratch += [
        vmem((9, 72, 128), f32),
        vmem((9, 72, 128), f32),
        vmem((9, 320, 192), bf16),
        vmem((9, 64, 192), bf16),
        vmem((9, 64, 192), bf16),
        vmem((9, 64, 192), bf16),
        vmem((9, 64, 576), bf16),
        vmem((9, 64, 192), bf16),
        vmem((9, 64, 128), f32),
        vmem((8, count), f32),
        vmem((128, count), bf16),
        vmem((3, 8, count), f32),
        vmem((3, 3, 128, count), bf16),
        vmem((3, 5, 128, count), bf16),
        vmem((3, 64, count), f32),
        vmem((3, 6, 64, count), f32),
        vmem((3, 7, 64, count), f32),
        vmem((8, count), f32),
        vmem((8, near), f32),
        vmem((128, near), bf16),
        vmem((8, near), f32),
        vmem((7, 64, near), f32),
        vmem((3, 256, near), bf16),
        vmem((5, 256, near), bf16),
        vmem((64, near), f32),
        vmem((6, 64, near), f32),
        vmem((7, 64, near), f32),
        vmem((8, near), f32),
        vmem((count, near), bf16),
        vmem((6, 72, 128), f32),
        vmem((plane, 8, 128), f32),
        vmem((sizes[2], 8, 128), f32),
        vmem((72, 128), f32),
        vmem((layers, sizes[2], 8, 128), f32),
        vmem((72, 128), f32),
    ]
    dma = pltpu.SemaphoreType.DMA
    scratch += [dma((12,))] + [dma((6,))] * 4
    scratch += [dma((number,)) for number in (TILES, plane, sizes[2], sizes[2], plane, TILES)]
    scratch += [dma((layers, sizes[2]))] * 4
    whole = pl.BlockSpec(memory_space=pltpu.VMEM)
    outside = pl.BlockSpec(memory_space=pltpu.HBM)
    results = pl.pallas_call(
        functools.partial(kernel, sizes),
        out_shape=[vmem(value.shape, value.dtype) for value in outs],
        in_specs=[outside] * 12,
        out_specs=[whole] * 11,
        scratch_shapes=scratch,
        compiler_params=pltpu.CompilerParams(
            collective_id=0, has_side_effects=True, vmem_limit_bytes=32 << 20
        ),
        cost_estimate=pl.CostEstimate(flops=500_000_000, bytes_accessed=1_000_000, transcendentals=400_000),
        name="training_step",
    )(*[pltpu.with_memory_space_constraint(value, pltpu.HBM) for value in operands])
    results = pl.pallas_call(
        hand_over,
        out_shape=outs,
        in_specs=[whole] * 11,
        out_specs=[outside] * 10 + [whole],
        scratch_shapes=[dma((10,))],
        compiler_params=pltpu.CompilerParams(vmem_limit_bytes=1 << 20),
        cost_estimate=pl.CostEstimate(flops=0, bytes_accessed=400_000, transcendentals=0),
        name="hand_over",
    )(*results)
    ranks = [params[k].shape for k in range(9)]
    arrays = [results[0].reshape(source.shape)]
    arrays += [value.reshape(shape) for value, shape in zip(results[1:10], ranks)]
    return tuple(arrays) + (results[10].reshape(()),)


def solution(mesh):
    sizes = tuple(mesh.shape[axis] for axis in AXES)
    cell = ("gx", "gy", "gz")
    column = ("gx", "gy")
    in_specs = (P(*cell, None, None), P(*cell, None, None), P(*cell, None))
    nets_specs = (
        (P(*cell, None, None), P(*cell, None, None, None), P(*cell, None, None))
        + (P(*column, None, None), P(*column, None, None, None), P(*column, None, None))
        + (P(), P(), P())
    )
    return jax.shard_map(
        functools.partial(step, sizes),
        mesh=mesh,
        in_specs=in_specs + nets_specs,
        out_specs=(P(*cell, None),) + nets_specs + (P(),),
        check_vma=False,
    )
```

```python
import functools

import jax
import jax.numpy as jnp
from jax import lax
from jax.experimental import pallas as pl
from jax.experimental.pallas import tpu as pltpu
from jax.sharding import PartitionSpec as P

MESH = pl.DeviceIdType.MESH
AXES = ("gx", "gy", "gz")
f32, bf16 = jnp.float32, jnp.bfloat16
wave_square = 4.0
inverse_depth = 8.0
TILES = 9
NT = (((1,), (1,)), ((), ()))


def split(value):
    high = value.astype(bf16)
    return high, (value - high.astype(f32)).astype(bf16)


def three(value):
    first = value.astype(bf16)
    rest = value - first.astype(f32)
    second = rest.astype(bf16)
    return first, second, (rest - second.astype(f32)).astype(bf16)


def left(matrix):
    high = matrix.astype(bf16).astype(f32)
    return jnp.concatenate([high, high, matrix - high], 1).astype(bf16)


def right(high, low):
    return jnp.concatenate([high, low, high], 0)


def dot(a, b):
    return jnp.dot(a, b, preferred_element_type=f32)


def dot_nt(a, b):
    return lax.dot_general(a, b, NT, preferred_element_type=f32)


def window(depth, facing):
    square = depth * depth
    smooth = depth * (15.0 - 10.0 * square + 3.0 * square * square) / 8.0
    blend = 0.5 * (1.0 - smooth)
    slope = (0.5 * inverse_depth * 15.0 / 8.0) * facing * (1.0 - square) * (1.0 - square)
    bend = (0.5 * inverse_depth * inverse_depth * 7.5) * depth * (1.0 - square)
    return blend, slope, bend


def tile_owners(sizes):
    chips = (sizes[1] + 1) // 2

    def order(place):
        x, chip = place // sizes[1], place % sizes[1] // 2
        return (x + chip + place) % 2, max(min(x, sizes[0] - x), min(chip, chips - chip)), place

    return sorted(range(sizes[0] * sizes[1]), key=order)[:TILES]


def far_first(sizes):
    def distance(offset):
        x, y = offset
        return -min(x, sizes[0] - x) - min(y, sizes[1] - y) / 2, x, y

    offsets = [(x, y) for x in range(sizes[0]) for y in range(sizes[1]) if x or y]
    return sorted(offsets, key=distance)


def kernel(sizes, *refs):
    (
        points_hbm,
        band_hbm,
        source_hbm,
        fine_first_hbm,
        fine_mid_hbm,
        fine_last_hbm,
        column_first_hbm,
        column_mid_hbm,
        column_last_hbm,
        global_first_hbm,
        global_mid_hbm,
        global_last_hbm,
        residual_out,
        fine_first_out,
        fine_mid_out,
        fine_last_out,
        column_first_out,
        column_mid_out,
        column_last_out,
        global_first_out,
        global_mid_out,
        global_last_out,
        loss_out,
        points,
        band,
        source,
        fine_first,
        fine_mid,
        fine_last,
        column_first,
        column_mid,
        column_last,
        global_first,
        global_mid,
        global_last,
        nets,
        grads,
        f1,
        f2,
        b2,
        b1h,
        b1s,
        b1p,
        cols,
        xp,
        xpb,
        alpha,
        x0,
        x1,
        h0s,
        a1,
        a2,
        res,
        xf,
        xfb,
        falpha,
        fcols,
        fx0,
        fx1,
        fh0s,
        fa1,
        fa2,
        fdelta,
        hot,
        back,
        tiles,
        levels,
        summed,
        columns,
        column_sum,
        load_sem,
        halo_send,
        halo_recv,
        back_send,
        back_recv,
        tile_send,
        tile_recv,
        level_send,
        level_recv,
        share_send,
        share_recv,
        column_send,
        column_recv,
        gather_send,
        gather_recv,
        relay,
    ) = refs
    me = tuple(lax.axis_index(axis) for axis in AXES)
    count = points.shape[2]
    slots = band.shape[2]
    pair = 2 * slots
    near = 6 * slots
    plane = sizes[0] * sizes[1]
    here = me[0] * sizes[1] + me[1]
    owners = tile_owners(sizes)
    reducer = here == owners[0]
    my_tile = jnp.int32(0)
    for tile in range(1, TILES):
        reducer = reducer | (here == owners[tile])
        my_tile = jnp.where(here == owners[tile], tile, my_tile)
    my_rows = pl.ds(pl.multiple_of(8 * my_tile, 8), 8)

    def peer(axis, offset):
        other = list(me)
        other[axis] = lax.rem(me[axis] + (offset + sizes[axis]), sizes[axis])
        return tuple(other)

    def in_plane(place):
        return (place // sizes[1], lax.rem(place, sizes[1]), me[2])

    def steps(axes, size):
        for axis in axes:
            if size <= sizes[axis] // 2:
                yield from {(axis, size), (axis, -size % sizes[axis])}

    circles = [sorted(steps((0, 1, 2), 1)), sorted(steps((0, 1, 2), 1)), sorted(steps((0, 1, 2), 2)), sorted(steps((1,), 4))]
    barrier = pltpu.get_barrier_semaphore()

    def semaphore_of(number):
        return relay.at[number - 1] if number else barrier

    def greet(number):
        for axis, step in circles[number]:
            pl.semaphore_signal(semaphore_of(number), inc=1, device_id=peer(axis, step), device_id_type=MESH)

    def hear(number):
        if circles[number]:
            pl.semaphore_wait(semaphore_of(number), len(circles[number]))

    greet(0)

    loads = [
        pltpu.make_async_copy(refs[k], refs[23 + k], load_sem.at[k])
        for k in (4, 3, 5, 0, 1, 2, 10, 9, 11, 7, 6, 8)
    ]
    for load in loads:
        load.start()

    def pack(net, first, mid, last):
        nets[net, 0:64, :] = jnp.concatenate([mid[0], mid[1]], 1)
        nets[net, 64:68, 0:64] = first[...]
        for k in range(3):
            nets[net, 68 + k : 69 + k, 0:64] = last[k] if len(last.shape) == 3 else last[k : k + 1, :]
        nets[net, 71:72, 0:64] = jnp.zeros((1, 64), f32)
        nets[net, 64:72, 64:128] = jnp.zeros((8, 64), f32)

    for load in loads[:3]:
        load.wait()
    pack(2, fine_first, fine_mid, fine_last)
    for load in loads[3:]:
        load.wait()
    pack(1, column_first, column_mid, column_last)
    pack(0, global_first, global_mid, global_last)

    def halo(face):
        axis, up = face // 2, face % 2
        return pltpu.make_async_remote_copy(
            src_ref=nets.at[2],
            dst_ref=nets.at[3 + (face ^ 1)],
            send_sem=halo_send.at[face],
            recv_sem=halo_recv.at[face ^ 1],
            device_id=peer(axis, 2 * up - 1),
            device_id_type=MESH,
        )

    faces = [face for face in range(6) if sizes[face // 2] > 1]
    place = [me[axis].astype(f32) for axis in range(3)]

    def affine(net):
        scale, shift = [], []
        for axis in range(3):
            fitted_scale = 2.0 / sizes[axis]
            fitted_shift = (2.0 * place[axis] + 1.0) * (1.0 / sizes[axis]) - 1.0
            fitted = (net == 0) if axis < 2 else (net <= 1)
            scale.append(jnp.where(fitted, fitted_scale, 2.0))
            shift.append(jnp.where(fitted, fitted_shift, 0.0))
        return scale, shift

    def face_affine(face):
        shift = [0.0, 0.0, 0.0]
        shift[face // 2] = 2.0 - 4.0 * (face % 2)
        return [2.0, 2.0, 2.0], shift

    def prepare_forward(net, scale, shift):
        mats = nets[net, 0:64, :]
        rows = nets[net, 64:72, :]
        turned = rows.T
        m1 = mats[:, 0:64]
        row = [scale[d] * rows[d : d + 1, 0:64] for d in range(3)]
        square = -2.0 * (row[0] * row[0] + row[1] * row[1] + row[2] * row[2])
        bias = turned[0:64, 3:4]
        for d in range(3):
            bias = bias + shift[d] * turned[0:64, d : d + 1]
        f1[net, 0:64, :] = left(m1)
        for d in range(3):
            f1[net, 64 * (d + 1) : 64 * (d + 2), :] = left(m1 * row[d])
        f1[net, 256:320, :] = left(m1 * square)
        f2[net] = left(mats[:, 64:128])
        lane = lax.broadcasted_iota(jnp.int32, (64, 8), 1)
        kept = turned[0:64, 0:8]
        for d in range(3):
            kept = jnp.where(lane == d, scale[d] * kept, kept)
        cols[net, :, 0:8] = jnp.where(lane == 3, bias, kept)

    def prepare_backward(net):
        turned = nets[net, 0:64, :].T
        m1t = turned[0:64]
        b1h[net] = left(m1t)
        col = [cols[net, :, d : d + 1] for d in range(3)]
        scaled = [m1t * col[d] for d in range(3)]
        high = [value.astype(bf16).astype(f32) for value in scaled]
        low = [scaled[d] - high[d] for d in range(3)]
        b1s[net] = jnp.concatenate(high + high + low, 1).astype(bf16)
        b1p[net] = left(m1t * (-2.0 * (col[0] * col[0] + col[1] * col[1] + col[2] * col[2])))
        b2[net] = left(turned[64:128])

    lane_ones = jnp.ones((1, count), f32)
    for d in range(3):
        xp[d : d + 1, :] = points[d]
    xp[3:4, :] = lane_ones
    xp[4:8, :] = jnp.zeros((4, count), f32)
    x_terms = three(xp[...])
    xpb[...] = jnp.zeros(xpb.shape, bf16)
    xpb[0:16, :] = jnp.concatenate([x_terms[0].astype(f32), x_terms[1].astype(f32)], 0).astype(bf16)

    def present(face):
        axis = face // 2
        there = me[axis] < sizes[axis] - 1 if face % 2 else me[axis] > 0
        return jnp.where(there, 1.0, 0.0).astype(f32)

    inside = lane_ones
    curve = jnp.zeros((1, count), f32)
    for axis in range(3):
        along = points[axis]
        upper = along > 0.0
        facing = jnp.where(upper, 1.0, -1.0)
        depth = jnp.minimum((0.5 - jnp.abs(along)) * inverse_depth, 1.0)
        exists = jnp.where(upper, present(2 * axis + 1), present(2 * axis))
        blend, slope, bend = window(depth, facing)
        inside = inside - exists * blend
        curve = curve - exists * bend
        alpha[2, 1 + axis : 2 + axis, :] = -2.0 * exists * slope
    alpha[2, 0:1, :] = wave_square * inside + curve
    alpha[2, 4:5, :] = inside
    for net in (0, 1):
        alpha[net, 0:1, :] = wave_square * lane_ones
        alpha[net, 1:4, :] = jnp.zeros((3, count), f32)
        alpha[net, 4:5, :] = lane_ones

    hear(0)
    for face in faces:
        halo(face).start()
    greet(1)

    near_lane = lax.broadcasted_iota(jnp.int32, (1, near), 1)
    face_of = near_lane // slots
    lower = lax.rem(face_of, 2) == 0
    stacked = jnp.concatenate([term.astype(f32) for term in x_terms], 0).astype(bf16)
    point_id = lax.broadcasted_iota(jnp.int32, (count, near), 0)
    listed = jnp.concatenate([band[face] for face in range(6)], 1)
    hot[...] = jnp.where(point_id == listed, 1.0, 0.0).astype(bf16)
    taken = dot(stacked, hot[...])
    taken = taken[0:8] + taken[8:16] + taken[16:24]
    xf[...] = taken
    high, low = split(taken)
    xfb[...] = jnp.zeros(xfb.shape, bf16)
    xfb[0:16, :] = jnp.concatenate([high.astype(f32), low.astype(f32)], 0).astype(bf16)
    facing = jnp.where(lower, -1.0, 1.0)
    axis_of = face_of // 2
    along = jnp.where(axis_of == 0, taken[0:1], jnp.where(axis_of == 1, taken[1:2], taken[2:3]))
    exists = jnp.zeros((1, near), f32)
    for face in range(6):
        exists = jnp.where(face_of == face, present(face), exists)
    depth = jnp.minimum((0.5 - facing * along) * inverse_depth, 1.0)
    blend, slope, bend = window(depth, facing)
    falpha[0:1, :] = exists * (wave_square * blend + bend)
    for d in range(3):
        falpha[1 + d : 2 + d, :] = jnp.where(axis_of == d, 2.0 * exists * slope, 0.0)
    falpha[4:5, :] = exists * blend

    def tanh_layer(z, f, m):
        h = jnp.tanh(z)
        s = 1.0 - h * h
        q = f[0] * f[0] + f[1] * f[1] + f[2] * f[2]
        return h, s, q, m - 2.0 * h * q

    def forward(get, x, al, mm, keep0, keep1, keep2):
        z = get(0) * x[0:1] + get(1) * x[1:2] + get(2) * x[2:3] + get(3)
        h = jnp.tanh(z)
        s = 1.0 - h * h
        p = h * s
        parts = [split(v) for v in (h, s, p)]
        keep0(h, parts)
        m1h = mm(f1, 0, 64, [right(*parts[0])])[0]
        m1f = mm(f1, 64, 256, [right(*parts[1])])[0]
        m1l = mm(f1, 256, 320, [right(*parts[2])])[0]
        f = [m1f[64 * d : 64 * (d + 1)] for d in range(3)]
        h, s, q, w = tanh_layer(m1h + get(4), f, m1l)
        parts = [split(v) for v in (h, s * f[0], s * f[1], s * f[2], s * w)]
        keep1((h, f[0], f[1], f[2], q, w), parts)
        out = mm(f2, 0, 64, [right(*part) for part in parts])
        f = out[1:4]
        h, s, q, w = tanh_layer(out[0] + get(5), f, out[4])
        u = al[1:2] * f[0] + al[2:3] * f[1] + al[3:4] * f[2] + al[4:5] * w
        c = al[0:1] * h + s * u
        keep2((h, f[0], f[1], f[2], q, u, c))
        return jnp.sum(get(6) * c, axis=0, keepdims=True)

    def backward(get, al, delta, mm, lane_sum, saved0, saved1, saved2):
        h, fa, fb, fc, q, u, c = saved2
        f = (fa, fb, fc)
        dlast = lane_sum(delta * c)
        e = get(6) * delta
        s = 1.0 - h * h
        es = e * s
        gm = es * al[4:5]
        k = 4.0 * h * gm
        gf = [es * al[1 + d : 2 + d] - k * f[d] for d in range(3)]
        gz = (e * al[0:1] - 2.0 * (q * gm + h * (e * u))) * s
        dbias1 = lane_sum(gz)
        g2 = [split(v) for v in (gz, gf[0], gf[1], gf[2], gm)]
        oh, oa, ob, oc, ol = mm(b2, 0, 64, [right(*part) for part in g2])
        o = (oa, ob, oc)
        h, fa, fb, fc, q, w = saved1
        f = (fa, fb, fc)
        s = 1.0 - h * h
        gm = ol * s
        k = 4.0 * h * gm
        gf = [o[d] * s - k * f[d] for d in range(3)]
        gs = o[0] * f[0] + o[1] * f[1] + o[2] * f[2] + ol * w
        gz = (oh - 2.0 * (q * gm + h * gs)) * s
        dbias0 = lane_sum(gz)
        g1 = [split(v) for v in (gz, gf[0], gf[1], gf[2], gm)]
        oh = mm(b1h, 0, 64, [right(*g1[0])])[0]
        os = mm(b1s, 0, 64, [jnp.concatenate([g1[d][k] for k in (0, 1, 0) for d in (1, 2, 3)], 0)])[0]
        op = mm(b1p, 0, 64, [right(*g1[4])])[0]
        h = saved0
        s = 1.0 - h * h
        gz = (oh + op * s - 2.0 * h * (os + op * h)) * s
        return g2, g1, split(gz), dlast, dbias1, dbias0

    def fold(product):
        return product[0:64] + product[64:128]

    def finish(net, scale, shift, dm2, ah, af, al, pts, dlast, dbias1, dbias0, extra):
        lane = lax.broadcasted_iota(jnp.int32, (64, 128), 1)
        pts = jnp.where(lane == 4, dbias0, pts)
        pts = jnp.where(lane == 5, dbias1, pts)
        pts = jnp.where(lane == 6, dlast, pts)
        turned = pts.T
        sums = turned[0:8] + turned[8:16]
        m1 = nets[net, 0:64, 0:64]
        rows = nets[net, 64:72, 0:64]
        row = [scale[d] * rows[d : d + 1] for d in range(3)]
        square = row[0] * row[0] + row[1] * row[1] + row[2] * row[2]
        dsquare = -2.0 * jnp.sum(m1 * al, axis=0, keepdims=True)
        dm1 = ah - 2.0 * (al * square)
        first = []
        for d in range(3):
            dm1 = dm1 + af[d] * row[d]
            slope = sums[d : d + 1] + jnp.sum(m1 * af[d], axis=0, keepdims=True) + 2.0 * row[d] * dsquare
            first.append(scale[d] * slope + shift[d] * sums[3:4])
        grads[net, 0:64, :] = jnp.concatenate([dm1, dm2], 1)
        grads[net, 64:72, 0:64] = jnp.concatenate(first + [sums[3:7], extra], 0)
        grads[net, 64:72, 64:128] = jnp.zeros((8, 64), f32)

    def wide_tools(net):
        def get(k):
            return cols[net, :, k : k + 1]

        def mm(ref, low, high, streams):
            out = dot(ref[net, low:high, :], jnp.concatenate(streams, 1))
            return [out[:, count * k : count * (k + 1)] for k in range(len(streams))]

        return get, mm

    def row_sums(value):
        return jnp.sum(value, axis=1, keepdims=True)

    def forward_wide(net):
        get, mm = wide_tools(net)

        def keep_parts(ref, parts):
            for k, part in enumerate(parts):
                ref[net, k, 0:64, :] = part[0]
                ref[net, k, 64:128, :] = part[1]

        def keep0(h, parts):
            h0s[net] = h
            keep_parts(x0, parts)

        def keep1(values, parts):
            for k, value in enumerate(values):
                a1[net, k] = value
            keep_parts(x1, parts)

        def keep2(values):
            for k, value in enumerate(values):
                a2[net, k] = value

        res[0:1, :] = res[0:1, :] + forward(get, xp[...], alpha[net], mm, keep0, keep1, keep2)

    def sides(value, low=0):
        return value[:, low : low + 64] + value[:, low + 64 : low + 128]

    def both(part):
        return jnp.concatenate(part, 0)

    def backward_wide(net, extra):
        get, mm = wide_tools(net)
        g2, g1, g0, dlast, dbias1, dbias0 = backward(
            get,
            alpha[net],
            res[1:2, :],
            mm,
            row_sums,
            h0s[net],
            [a1[net, k] for k in range(6)],
            [a2[net, k] for k in range(7)],
        )
        dm2 = dot_nt(
            jnp.concatenate([both(g) for g in g2], 1),
            jnp.concatenate([x1[net, k] for k in range(5)], 1),
        )
        ah = dot_nt(both(g1[0]), x0[net, 0])
        af = dot_nt(jnp.concatenate([both(g) for g in g1[1:4]], 0), x0[net, 1])
        al = dot_nt(both(g1[4]), x0[net, 2])
        pts = fold(dot_nt(both(g0), xpb[...]))
        af = [sides(fold(af[128 * d : 128 * (d + 1)])) for d in range(3)]
        scale, shift = affine(net)
        dm2, ah, al = [sides(fold(value)) for value in (dm2, ah, al)]
        finish(net, scale, shift, dm2, ah, af, al, pts, dlast, dbias1, dbias0, extra)

    half = lax.broadcasted_iota(jnp.int32, (1, pair), 1) < slots
    first_half = jnp.where(lower, 1.0, 0.0).astype(bf16)
    second_half = jnp.where(lower, 0.0, 1.0).astype(bf16)

    def face_get(k):
        return fcols[k]

    def face_mm(ref, low, high, streams):
        rows = high - low
        number = len(streams)
        mask = (lax.broadcasted_iota(jnp.int32, (1, number * pair), 1) & (pair - 1)) < slots
        pieces = []
        for axis in range(3):
            net = 3 + 2 * axis
            span = slice(axis * pair, (axis + 1) * pair)
            lhs = jnp.concatenate([ref[net, low:high, :], ref[net + 1, low:high, :]], 0)
            out = dot(lhs, jnp.concatenate([stream[:, span] for stream in streams], 1))
            out = jnp.where(mask, out[0:rows], out[rows : 2 * rows])
            pieces.append([out[:, pair * k : pair * (k + 1)] for k in range(number)])
        return [jnp.concatenate([piece[k] for piece in pieces], 1) for k in range(number)]

    def half_sums(value):
        return [
            row_sums(jnp.where(half if face % 2 == 0 else ~half, value[:, pair * (face // 2) : pair * (face // 2 + 1)], 0.0))
            for face in range(6)
        ]

    def forward_faces():
        def keep_parts(ref, parts):
            for k, part in enumerate(parts):
                ref[k, 0:64, :] = part[0] * first_half
                ref[k, 64:128, :] = part[1] * first_half
                ref[k, 128:192, :] = part[0] * second_half
                ref[k, 192:256, :] = part[1] * second_half

        def keep0(h, parts):
            fh0s[...] = h
            keep_parts(fx0, parts)

        def keep1(values, parts):
            for k, value in enumerate(values):
                fa1[k] = value
            keep_parts(fx1, parts)

        def keep2(values):
            for k, value in enumerate(values):
                fa2[k] = value

        row = forward(face_get, xf[...], falpha[...], face_mm, keep0, keep1, keep2)
        terms = jnp.concatenate([term.astype(f32) for term in three(row)] + [jnp.zeros((5, near), f32)], 0)
        spread = dot_nt(terms.astype(bf16), hot[...])
        res[0:1, :] = res[0:1, :] + (spread[0:1] + spread[1:2] + spread[2:3])

    def backward_faces():
        g2, g1, g0, dlast, dbias1, dbias0 = backward(
            face_get,
            falpha[...],
            fdelta[0:1, :],
            face_mm,
            half_sums,
            fh0s[...],
            [fa1[k] for k in range(6)],
            [fa2[k] for k in range(7)],
        )
        for axis in range(3):
            span = slice(axis * pair, (axis + 1) * pair)

            def cut(part):
                return jnp.concatenate([part[0][:, span], part[1][:, span]], 0)

            dm2 = fold(
                dot_nt(
                    jnp.concatenate([cut(g) for g in g2], 1),
                    jnp.concatenate([fx1[k, :, span] for k in range(5)], 1),
                )
            )
            ah = fold(dot_nt(cut(g1[0]), fx0[0, :, span]))
            af = dot_nt(jnp.concatenate([cut(g) for g in g1[1:4]], 0), fx0[1, :, span])
            af = [fold(af[128 * d : 128 * (d + 1)]) for d in range(3)]
            al = fold(dot_nt(cut(g1[4]), fx0[2, :, span]))
            for side in range(2):
                face = 2 * axis + side
                kept = (first_half if side == 0 else second_half)[:, span]
                pts = fold(dot_nt(cut(g0), xfb[:, span] * kept))
                scale, shift = face_affine(face)
                finish(
                    3 + face,
                    scale,
                    shift,
                    sides(dm2, 128 * side),
                    sides(ah, 128 * side),
                    [sides(v, 128 * side) for v in af],
                    sides(al, 128 * side),
                    pts,
                    dlast[face],
                    dbias1[face],
                    dbias0[face],
                    jnp.zeros((1, 64), f32),
                )

    def total(ref, number):
        value = ref[0]
        for k in range(1, number):
            value = value + ref[k]
        return value

    def tile_copy(tile):
        return pltpu.make_async_remote_copy(
            src_ref=grads.at[0, 8 * tile : 8 * tile + 8, :],
            dst_ref=tiles.at[here],
            send_sem=tile_send.at[tile],
            recv_sem=tile_recv.at[here],
            device_id=(owners[tile] // sizes[1], owners[tile] % sizes[1], me[2]),
            device_id_type=MESH,
        )

    def tile_arrival(sender):
        return pltpu.make_async_remote_copy(
            src_ref=grads.at[0, 0:8, :],
            dst_ref=tiles.at[sender],
            send_sem=tile_send.at[0],
            recv_sem=tile_recv.at[sender],
            device_id=in_plane(sender),
            device_id_type=MESH,
        )

    def along_z(source_ref, ref, send, recv, offset, sender):
        return pltpu.make_async_remote_copy(
            src_ref=source_ref,
            dst_ref=ref.at[sender],
            send_sem=send.at[offset],
            recv_sem=recv.at[sender],
            device_id=peer(2, offset),
            device_id_type=MESH,
        )

    def level_copy(offset, arriving):
        sender = lax.rem(me[2] + (sizes[2] - offset), sizes[2]) if arriving else me[2]
        return along_z(levels.at[me[2]], levels, level_send, level_recv, offset, sender)

    layers = -(-TILES // sizes[2])

    def column_copies(offset, arriving):
        target = lax.rem(me[2] + offset, sizes[2])
        sender = lax.rem(me[2] + (sizes[2] - offset), sizes[2]) if arriving else me[2]
        for layer in range(layers):
            tile = layer * sizes[2] + (me[2] if arriving else target)
            rows = pl.ds(pl.multiple_of(8 * lax.rem(tile, TILES), 8), 8)
            yield tile < TILES, pltpu.make_async_remote_copy(
                src_ref=grads.at[1, rows, :],
                dst_ref=columns.at[layer, sender],
                send_sem=column_send.at[layer, offset],
                recv_sem=column_recv.at[layer, sender],
                device_id=peer(2, offset),
                device_id_type=MESH,
            )

    def gather_copies(offset, arriving):
        sender = lax.rem(me[2] + (sizes[2] - offset), sizes[2]) if arriving else me[2]
        for layer in range(layers):
            tile = layer * sizes[2] + sender
            rows = pl.ds(pl.multiple_of(8 * lax.rem(tile, TILES), 8), 8)
            yield tile < TILES, pltpu.make_async_remote_copy(
                src_ref=column_sum.at[rows, :],
                dst_ref=column_sum.at[rows, :],
                send_sem=gather_send.at[layer, offset],
                recv_sem=gather_recv.at[layer, sender],
                device_id=peer(2, offset),
                device_id_type=MESH,
            )

    def own_layers():
        for layer in range(layers):
            tile = layer * sizes[2] + me[2]
            yield layer, tile < TILES, pl.ds(pl.multiple_of(8 * lax.rem(tile, TILES), 8), 8)

    def every(copies, arriving, action):
        for offset in range(1, sizes[2]):
            for needed, copy in copies(offset, arriving):
                pl.when(needed)(getattr(copy, action))

    def share_copy(number):
        x, y = far_first(sizes)[number]
        target = (lax.rem(me[0] + x, sizes[0]), lax.rem(me[1] + y, sizes[1]), me[2])
        return pltpu.make_async_remote_copy(
            src_ref=summed.at[my_rows, :],
            dst_ref=summed.at[my_rows, :],
            send_sem=share_send.at[number],
            recv_sem=share_recv.at[my_tile],
            device_id=target,
            device_id_type=MESH,
        )

    def share_arrival(tile):
        rows = summed.at[8 * tile : 8 * tile + 8, :]
        return pltpu.make_async_remote_copy(
            src_ref=rows,
            dst_ref=rows,
            send_sem=share_send.at[0],
            recv_sem=share_recv.at[tile],
            device_id=in_plane(owners[tile]),
            device_id_type=MESH,
        )

    def send_back(face):
        axis, up = face // 2, face % 2
        return pltpu.make_async_remote_copy(
            src_ref=grads.at[3 + face],
            dst_ref=back.at[face ^ 1],
            send_sem=back_send.at[face],
            recv_sem=back_recv.at[face ^ 1],
            device_id=peer(axis, 2 * up - 1),
            device_id_type=MESH,
        )

    def give(value, first_ref, mid_ref, last_ref):
        mid_ref[0] = value[0:64, 0:64]
        mid_ref[1] = value[0:64, 64:128]
        first_ref[...] = value[64:68, 0:64]
        for k in range(3):
            if len(last_ref.shape) == 3:
                last_ref[k] = value[68 + k : 69 + k, 0:64]
            else:
                last_ref[k : k + 1, :] = value[68 + k : 69 + k, 0:64]

    res[0:1, :] = -source[...]

    for net in range(3):
        prepare_forward(net, *affine(net))
        forward_wide(net)
        if net == 0:
            hear(1)
            greet(2)
    hear(2)
    greet(3)
    prepare_backward(0)
    for face in faces:
        halo(face).wait()
    for face in range(6):
        prepare_forward(3 + face, *face_affine(face))
    for k in range(7):
        fcols[k] = jnp.concatenate(
            [
                jnp.where(half, cols[3 + 2 * axis, :, k : k + 1], cols[4 + 2 * axis, :, k : k + 1])
                for axis in range(3)
            ],
            1,
        )
    forward_faces()

    residual = res[0:1, :]
    residual_out[...] = residual
    delta = residual * (1.0 / count)
    res[1:2, :] = delta
    loss = jnp.sum(residual * residual, axis=1, keepdims=True) * (0.5 / count)

    first_lane = lax.broadcasted_iota(jnp.int32, (1, 64), 1) == 0
    backward_wide(0, jnp.where(first_lane, loss, 0.0))
    hear(3)
    for tile in range(TILES):
        pl.when(here != owners[tile])(tile_copy(tile).start)

    prepare_backward(1)
    backward_wide(1, jnp.zeros((1, 64), f32))
    every(column_copies, False, "start")

    terms = jnp.concatenate([term.astype(f32) for term in three(delta)] + [jnp.zeros((5, count), f32)], 0)
    taken = dot(terms.astype(bf16), hot[...])
    fdelta[0:1, :] = taken[0:1] + taken[1:2] + taken[2:3]

    for face in range(6):
        prepare_backward(3 + face)
    backward_faces()
    for face in faces:
        send_back(face).start()

    @pl.when(reducer)
    def _():
        tiles[here] = grads[0, my_rows, :]
        for offset in range(1, plane):
            tile_arrival(lax.rem(here + offset, plane)).wait_recv()
        levels[me[2]] = total(tiles, plane)
        for offset in range(1, sizes[2]):
            level_copy(offset, False).start()

    prepare_backward(2)
    backward_wide(2, jnp.zeros((1, 64), f32))

    for layer, needed, rows in own_layers():

        @pl.when(needed)
        def _(layer=layer, rows=rows):
            columns[layer, me[2]] = grads[1, rows, :]

    every(column_copies, True, "wait_recv")
    for layer, needed, rows in own_layers():

        @pl.when(needed)
        def _(layer=layer, rows=rows):
            column_sum[rows, :] = total(columns.at[layer], sizes[2])

    every(gather_copies, False, "start")

    for face in faces:
        send_back(face).wait()
    give(grads[2] + total(back, 6), fine_first_out, fine_mid_out, fine_last_out)

    @pl.when(reducer)
    def _():
        for offset in range(1, sizes[2]):
            level_copy(offset, True).wait_recv()
        summed[my_rows, :] = total(levels, sizes[2])
        for number in range(plane - 1):
            share_copy(number).start()

    every(gather_copies, True, "wait_recv")
    give(column_sum[...], column_first_out, column_mid_out, column_last_out)
    every(column_copies, False, "wait_send")
    every(gather_copies, False, "wait_send")
    for tile in range(TILES):
        pl.when(here != owners[tile])(tile_copy(tile).wait_send)
    for tile in range(TILES):
        pl.when(here != owners[tile])(share_arrival(tile).wait_recv)
    value = summed[...]
    give(value, global_first_out, global_mid_out, global_last_out)
    loss_out[...] = value[71:72, 0:1]

    @pl.when(reducer)
    def _():
        for offset in range(1, sizes[2]):
            level_copy(offset, False).wait_send()
        for number in range(plane - 1):
            share_copy(number).wait_send()


def hand_over(*refs):
    number = len(refs) // 2
    ins, outs, sem = refs[:number], refs[number : 2 * number], refs[2 * number]
    copies = [pltpu.make_async_copy(ins[k], outs[k], sem.at[k]) for k in range(number - 1)]
    for copy in copies:
        copy.start()
    outs[number - 1][...] = ins[number - 1][...]
    for copy in copies:
        copy.wait()


def step(sizes, points, band_index, source, *params):
    count = points.shape[-1]
    slots = band_index.shape[-1]
    near = 6 * slots
    plane = sizes[0] * sizes[1]
    layers = -(-TILES // sizes[2])
    operands = [points.reshape(3, 1, count), band_index.reshape(6, 1, slots), source.reshape(1, count)]
    shapes = [(4, 64), (2, 64, 64), (3, 1, 64)] * 2 + [(4, 64), (2, 64, 64), (3, 64)]
    operands += [param.reshape(shape) for param, shape in zip(params, shapes)]
    outs = [jax.ShapeDtypeStruct(shape, f32) for shape in [(1, count)] + shapes + [(1, 1)]]
    vmem = pltpu.VMEM
    scratch = [vmem(value.shape, value.dtype) for value in operands]
    scratch += [
        vmem((9, 72, 128), f32),
        vmem((9, 72, 128), f32),
        vmem((9, 320, 192), bf16),
        vmem((9, 64, 192), bf16),
        vmem((9, 64, 192), bf16),
        vmem((9, 64, 192), bf16),
        vmem((9, 64, 576), bf16),
        vmem((9, 64, 192), bf16),
        vmem((9, 64, 128), f32),
        vmem((8, count), f32),
        vmem((128, count), bf16),
        vmem((3, 8, count), f32),
        vmem((3, 3, 128, count), bf16),
        vmem((3, 5, 128, count), bf16),
        vmem((3, 64, count), f32),
        vmem((3, 6, 64, count), f32),
        vmem((3, 7, 64, count), f32),
        vmem((8, count), f32),
        vmem((8, near), f32),
        vmem((128, near), bf16),
        vmem((8, near), f32),
        vmem((7, 64, near), f32),
        vmem((3, 256, near), bf16),
        vmem((5, 256, near), bf16),
        vmem((64, near), f32),
        vmem((6, 64, near), f32),
        vmem((7, 64, near), f32),
        vmem((8, near), f32),
        vmem((count, near), bf16),
        vmem((6, 72, 128), f32),
        vmem((plane, 8, 128), f32),
        vmem((sizes[2], 8, 128), f32),
        vmem((72, 128), f32),
        vmem((layers, sizes[2], 8, 128), f32),
        vmem((72, 128), f32),
    ]
    dma = pltpu.SemaphoreType.DMA
    scratch += [dma((12,))] + [dma((6,))] * 4
    scratch += [dma((number,)) for number in (TILES, plane, sizes[2], sizes[2], plane, TILES)]
    scratch += [dma((layers, sizes[2]))] * 4 + [pltpu.SemaphoreType.REGULAR((3,))]
    whole = pl.BlockSpec(memory_space=pltpu.VMEM)
    outside = pl.BlockSpec(memory_space=pltpu.HBM)
    results = pl.pallas_call(
        functools.partial(kernel, sizes),
        out_shape=[vmem(value.shape, value.dtype) for value in outs],
        in_specs=[outside] * 12,
        out_specs=[whole] * 11,
        scratch_shapes=scratch,
        compiler_params=pltpu.CompilerParams(
            collective_id=0, has_side_effects=True, vmem_limit_bytes=32 << 20
        ),
        cost_estimate=pl.CostEstimate(flops=500_000_000, bytes_accessed=1_000_000, transcendentals=400_000),
        name="training_step",
    )(*[pltpu.with_memory_space_constraint(value, pltpu.HBM) for value in operands])
    results = pl.pallas_call(
        hand_over,
        out_shape=outs,
        in_specs=[whole] * 11,
        out_specs=[outside] * 10 + [whole],
        scratch_shapes=[dma((10,))],
        compiler_params=pltpu.CompilerParams(vmem_limit_bytes=1 << 20),
        cost_estimate=pl.CostEstimate(flops=0, bytes_accessed=400_000, transcendentals=0),
        name="hand_over",
    )(*results)
    ranks = [params[k].shape for k in range(9)]
    arrays = [results[0].reshape(source.shape)]
    arrays += [value.reshape(shape) for value, shape in zip(results[1:10], ranks)]
    return tuple(arrays) + (results[10].reshape(()),)


def solution(mesh):
    sizes = tuple(mesh.shape[axis] for axis in AXES)
    cell = ("gx", "gy", "gz")
    column = ("gx", "gy")
    in_specs = (P(*cell, None, None), P(*cell, None, None), P(*cell, None))
    nets_specs = (
        (P(*cell, None, None), P(*cell, None, None, None), P(*cell, None, None))
        + (P(*column, None, None), P(*column, None, None, None), P(*column, None, None))
        + (P(), P(), P())
    )
    return jax.shard_map(
        functools.partial(step, sizes),
        mesh=mesh,
        in_specs=in_specs + nets_specs,
        out_specs=(P(*cell, None),) + nets_specs + (P(),),
        check_vma=False,
    )
```

```python
import functools

import jax
import jax.numpy as jnp
from jax import lax
from jax.experimental import pallas as pl
from jax.experimental.pallas import tpu as pltpu
from jax.sharding import PartitionSpec as P

MESH = pl.DeviceIdType.MESH
AXES = ("gx", "gy", "gz")
f32, bf16 = jnp.float32, jnp.bfloat16
wave_square = 4.0
inverse_depth = 8.0
TILES = 9
NT = (((1,), (1,)), ((), ()))


def split(value):
    high = value.astype(bf16)
    return high, (value - high.astype(f32)).astype(bf16)


def three(value):
    first = value.astype(bf16)
    rest = value - first.astype(f32)
    second = rest.astype(bf16)
    return first, second, (rest - second.astype(f32)).astype(bf16)


def left(matrix):
    high = matrix.astype(bf16).astype(f32)
    return jnp.concatenate([high, high, matrix - high], 1).astype(bf16)


def right(high, low):
    return jnp.concatenate([high, low, high], 0)


def dot(a, b):
    return jnp.dot(a, b, preferred_element_type=f32)


def dot_nt(a, b):
    return lax.dot_general(a, b, NT, preferred_element_type=f32)


def window(depth, facing):
    square = depth * depth
    smooth = depth * (15.0 - 10.0 * square + 3.0 * square * square) / 8.0
    blend = 0.5 * (1.0 - smooth)
    slope = (0.5 * inverse_depth * 15.0 / 8.0) * facing * (1.0 - square) * (1.0 - square)
    bend = (0.5 * inverse_depth * inverse_depth * 7.5) * depth * (1.0 - square)
    return blend, slope, bend


def tile_owners(sizes):
    chips = (sizes[1] + 1) // 2

    def order(place):
        x, chip = place // sizes[1], place % sizes[1] // 2
        return (x + chip + place) % 2, max(min(x, sizes[0] - x), min(chip, chips - chip)), place

    return sorted(range(sizes[0] * sizes[1]), key=order)[:TILES]


def far_first(sizes):
    def distance(offset):
        x, y = offset
        return -min(x, sizes[0] - x) - min(y, sizes[1] - y) / 2, x, y

    offsets = [(x, y) for x in range(sizes[0]) for y in range(sizes[1]) if x or y]
    return sorted(offsets, key=distance)


def kernel(sizes, *refs):
    (
        points_hbm,
        band_hbm,
        source_hbm,
        fine_first_hbm,
        fine_mid_hbm,
        fine_last_hbm,
        column_first_hbm,
        column_mid_hbm,
        column_last_hbm,
        global_first_hbm,
        global_mid_hbm,
        global_last_hbm,
        residual_out,
        fine_first_out,
        fine_mid_out,
        fine_last_out,
        column_first_out,
        column_mid_out,
        column_last_out,
        global_first_out,
        global_mid_out,
        global_last_out,
        loss_out,
        points,
        band,
        source,
        fine_first,
        fine_mid,
        fine_last,
        column_first,
        column_mid,
        column_last,
        global_first,
        global_mid,
        global_last,
        nets,
        grads,
        f1,
        f2,
        b2,
        b1h,
        b1s,
        b1p,
        cols,
        xp,
        xpb,
        alpha,
        x0,
        x1,
        h0s,
        a1,
        a2,
        res,
        xf,
        xfb,
        falpha,
        fcols,
        fx0,
        fx1,
        fh0s,
        fa1,
        fa2,
        fdelta,
        hot,
        back,
        tiles,
        levels,
        summed,
        columns,
        column_sum,
        load_sem,
        halo_send,
        halo_recv,
        back_send,
        back_recv,
        tile_send,
        tile_recv,
        level_send,
        level_recv,
        share_send,
        share_recv,
        column_send,
        column_recv,
        gather_send,
        gather_recv,
        relay,
    ) = refs
    me = tuple(lax.axis_index(axis) for axis in AXES)
    count = points.shape[2]
    slots = band.shape[2]
    pair = 2 * slots
    near = 6 * slots
    plane = sizes[0] * sizes[1]
    here = me[0] * sizes[1] + me[1]
    owners = tile_owners(sizes)
    reducer = here == owners[0]
    my_tile = jnp.int32(0)
    for tile in range(1, TILES):
        reducer = reducer | (here == owners[tile])
        my_tile = jnp.where(here == owners[tile], tile, my_tile)
    my_rows = pl.ds(pl.multiple_of(8 * my_tile, 8), 8)

    def peer(axis, offset):
        other = list(me)
        other[axis] = lax.rem(me[axis] + (offset + sizes[axis]), sizes[axis])
        return tuple(other)

    def in_plane(place):
        return (place // sizes[1], lax.rem(place, sizes[1]), me[2])

    def steps(axes, size):
        for axis in axes:
            if size <= sizes[axis] // 2:
                yield from {(axis, size), (axis, -size % sizes[axis])}

    circles = [sorted(steps((0, 1, 2), 1)), sorted(steps((0, 1, 2), 1)), sorted(steps((0, 1, 2), 2)), sorted(steps((1,), 4))]
    barrier = pltpu.get_barrier_semaphore()

    def semaphore_of(number):
        return relay.at[number - 1] if number else barrier

    def greet(number):
        for axis, step in circles[number]:
            pl.semaphore_signal(semaphore_of(number), inc=1, device_id=peer(axis, step), device_id_type=MESH)

    def hear(number):
        if circles[number]:
            pl.semaphore_wait(semaphore_of(number), len(circles[number]))

    greet(0)

    loads = [
        pltpu.make_async_copy(refs[k], refs[23 + k], load_sem.at[k])
        for k in (4, 3, 5, 0, 1, 2, 10, 9, 11, 7, 6, 8)
    ]
    for load in loads:
        load.start()

    def pack(net, first, mid, last):
        nets[net, 0:64, :] = jnp.concatenate([mid[0], mid[1]], 1)
        nets[net, 64:68, 0:64] = first[...]
        for k in range(3):
            nets[net, 68 + k : 69 + k, 0:64] = last[k] if len(last.shape) == 3 else last[k : k + 1, :]
        nets[net, 71:72, 0:64] = jnp.zeros((1, 64), f32)
        nets[net, 64:72, 64:128] = jnp.zeros((8, 64), f32)

    for load in loads[:3]:
        load.wait()
    pack(2, fine_first, fine_mid, fine_last)
    for load in loads[3:]:
        load.wait()
    pack(1, column_first, column_mid, column_last)
    pack(0, global_first, global_mid, global_last)

    def halo(face):
        axis, up = face // 2, face % 2
        return pltpu.make_async_remote_copy(
            src_ref=nets.at[2],
            dst_ref=nets.at[3 + (face ^ 1)],
            send_sem=halo_send.at[face],
            recv_sem=halo_recv.at[face ^ 1],
            device_id=peer(axis, 2 * up - 1),
            device_id_type=MESH,
        )

    faces = [face for face in range(6) if sizes[face // 2] > 1]
    place = [me[axis].astype(f32) for axis in range(3)]

    def affine(net):
        scale, shift = [], []
        for axis in range(3):
            fitted_scale = 2.0 / sizes[axis]
            fitted_shift = (2.0 * place[axis] + 1.0) * (1.0 / sizes[axis]) - 1.0
            fitted = (net == 0) if axis < 2 else (net <= 1)
            scale.append(jnp.where(fitted, fitted_scale, 2.0))
            shift.append(jnp.where(fitted, fitted_shift, 0.0))
        return scale, shift

    def face_affine(face):
        shift = [0.0, 0.0, 0.0]
        shift[face // 2] = 2.0 - 4.0 * (face % 2)
        return [2.0, 2.0, 2.0], shift

    def prepare_forward(net, scale, shift):
        mats = nets[net, 0:64, :]
        rows = nets[net, 64:72, :]
        turned = rows.T
        m1 = mats[:, 0:64]
        row = [scale[d] * rows[d : d + 1, 0:64] for d in range(3)]
        square = -2.0 * (row[0] * row[0] + row[1] * row[1] + row[2] * row[2])
        bias = turned[0:64, 3:4]
        for d in range(3):
            bias = bias + shift[d] * turned[0:64, d : d + 1]
        f1[net, 0:64, :] = left(m1)
        for d in range(3):
            f1[net, 64 * (d + 1) : 64 * (d + 2), :] = left(m1 * row[d])
        f1[net, 256:320, :] = left(m1 * square)
        f2[net] = left(mats[:, 64:128])
        lane = lax.broadcasted_iota(jnp.int32, (64, 8), 1)
        kept = turned[0:64, 0:8]
        for d in range(3):
            kept = jnp.where(lane == d, scale[d] * kept, kept)
        cols[net, :, 0:8] = jnp.where(lane == 3, bias, kept)

    def prepare_backward(net):
        turned = nets[net, 0:64, :].T
        m1t = turned[0:64]
        b1h[net] = left(m1t)
        col = [cols[net, :, d : d + 1] for d in range(3)]
        scaled = [m1t * col[d] for d in range(3)]
        high = [value.astype(bf16).astype(f32) for value in scaled]
        low = [scaled[d] - high[d] for d in range(3)]
        b1s[net] = jnp.concatenate(high + high + low, 1).astype(bf16)
        b1p[net] = left(m1t * (-2.0 * (col[0] * col[0] + col[1] * col[1] + col[2] * col[2])))
        b2[net] = left(turned[64:128])

    lane_ones = jnp.ones((1, count), f32)
    for d in range(3):
        xp[d : d + 1, :] = points[d]
    xp[3:4, :] = lane_ones
    xp[4:8, :] = jnp.zeros((4, count), f32)
    x_terms = three(xp[...])
    xpb[...] = jnp.zeros(xpb.shape, bf16)
    xpb[0:16, :] = jnp.concatenate([x_terms[0].astype(f32), x_terms[1].astype(f32)], 0).astype(bf16)

    def present(face):
        axis = face // 2
        there = me[axis] < sizes[axis] - 1 if face % 2 else me[axis] > 0
        return jnp.where(there, 1.0, 0.0).astype(f32)

    inside = lane_ones
    curve = jnp.zeros((1, count), f32)
    for axis in range(3):
        along = points[axis]
        upper = along > 0.0
        facing = jnp.where(upper, 1.0, -1.0)
        depth = jnp.minimum((0.5 - jnp.abs(along)) * inverse_depth, 1.0)
        exists = jnp.where(upper, present(2 * axis + 1), present(2 * axis))
        blend, slope, bend = window(depth, facing)
        inside = inside - exists * blend
        curve = curve - exists * bend
        alpha[2, 1 + axis : 2 + axis, :] = -2.0 * exists * slope
    alpha[2, 0:1, :] = wave_square * inside + curve
    alpha[2, 4:5, :] = inside
    for net in (0, 1):
        alpha[net, 0:1, :] = wave_square * lane_ones
        alpha[net, 1:4, :] = jnp.zeros((3, count), f32)
        alpha[net, 4:5, :] = lane_ones

    hear(0)
    for face in faces:
        halo(face).start()
    greet(1)

    near_lane = lax.broadcasted_iota(jnp.int32, (1, near), 1)
    face_of = near_lane // slots
    lower = lax.rem(face_of, 2) == 0
    stacked = jnp.concatenate([term.astype(f32) for term in x_terms], 0).astype(bf16)
    point_id = lax.broadcasted_iota(jnp.int32, (count, near), 0)
    listed = jnp.concatenate([band[face] for face in range(6)], 1)
    hot[...] = jnp.where(point_id == listed, 1.0, 0.0).astype(bf16)
    taken = dot(stacked, hot[...])
    taken = taken[0:8] + taken[8:16] + taken[16:24]
    xf[...] = taken
    high, low = split(taken)
    xfb[...] = jnp.zeros(xfb.shape, bf16)
    xfb[0:16, :] = jnp.concatenate([high.astype(f32), low.astype(f32)], 0).astype(bf16)
    facing = jnp.where(lower, -1.0, 1.0)
    axis_of = face_of // 2
    along = jnp.where(axis_of == 0, taken[0:1], jnp.where(axis_of == 1, taken[1:2], taken[2:3]))
    exists = jnp.zeros((1, near), f32)
    for face in range(6):
        exists = jnp.where(face_of == face, present(face), exists)
    depth = jnp.minimum((0.5 - facing * along) * inverse_depth, 1.0)
    blend, slope, bend = window(depth, facing)
    falpha[0:1, :] = exists * (wave_square * blend + bend)
    for d in range(3):
        falpha[1 + d : 2 + d, :] = jnp.where(axis_of == d, 2.0 * exists * slope, 0.0)
    falpha[4:5, :] = exists * blend

    def tanh_layer(z, f, m):
        h = jnp.tanh(z)
        s = 1.0 - h * h
        q = f[0] * f[0] + f[1] * f[1] + f[2] * f[2]
        return h, s, q, m - 2.0 * h * q

    def forward(get, x, al, mm, keep0, keep1, keep2):
        z = get(0) * x[0:1] + get(1) * x[1:2] + get(2) * x[2:3] + get(3)
        h = jnp.tanh(z)
        s = 1.0 - h * h
        p = h * s
        parts = [split(v) for v in (h, s, p)]
        keep0(h, parts)
        m1h = mm(f1, 0, 64, [right(*parts[0])])[0]
        m1f = mm(f1, 64, 256, [right(*parts[1])])[0]
        m1l = mm(f1, 256, 320, [right(*parts[2])])[0]
        f = [m1f[64 * d : 64 * (d + 1)] for d in range(3)]
        h, s, q, w = tanh_layer(m1h + get(4), f, m1l)
        parts = [split(v) for v in (h, s * f[0], s * f[1], s * f[2], s * w)]
        keep1((h, f[0], f[1], f[2], q, w), parts)
        out = mm(f2, 0, 64, [right(*part) for part in parts])
        f = out[1:4]
        h, s, q, w = tanh_layer(out[0] + get(5), f, out[4])
        u = al[1:2] * f[0] + al[2:3] * f[1] + al[3:4] * f[2] + al[4:5] * w
        c = al[0:1] * h + s * u
        keep2((h, f[0], f[1], f[2], q, u, c))
        return jnp.sum(get(6) * c, axis=0, keepdims=True)

    def backward(get, al, delta, mm, lane_sum, saved0, saved1, saved2):
        h, fa, fb, fc, q, u, c = saved2
        f = (fa, fb, fc)
        dlast = lane_sum(delta * c)
        e = get(6) * delta
        s = 1.0 - h * h
        es = e * s
        gm = es * al[4:5]
        k = 4.0 * h * gm
        gf = [es * al[1 + d : 2 + d] - k * f[d] for d in range(3)]
        gz = (e * al[0:1] - 2.0 * (q * gm + h * (e * u))) * s
        dbias1 = lane_sum(gz)
        g2 = [split(v) for v in (gz, gf[0], gf[1], gf[2], gm)]
        oh, oa, ob, oc, ol = mm(b2, 0, 64, [right(*part) for part in g2])
        o = (oa, ob, oc)
        h, fa, fb, fc, q, w = saved1
        f = (fa, fb, fc)
        s = 1.0 - h * h
        gm = ol * s
        k = 4.0 * h * gm
        gf = [o[d] * s - k * f[d] for d in range(3)]
        gs = o[0] * f[0] + o[1] * f[1] + o[2] * f[2] + ol * w
        gz = (oh - 2.0 * (q * gm + h * gs)) * s
        dbias0 = lane_sum(gz)
        g1 = [split(v) for v in (gz, gf[0], gf[1], gf[2], gm)]
        oh = mm(b1h, 0, 64, [right(*g1[0])])[0]
        os = mm(b1s, 0, 64, [jnp.concatenate([g1[d][k] for k in (0, 1, 0) for d in (1, 2, 3)], 0)])[0]
        op = mm(b1p, 0, 64, [right(*g1[4])])[0]
        h = saved0
        s = 1.0 - h * h
        gz = (oh + op * s - 2.0 * h * (os + op * h)) * s
        return g2, g1, split(gz), dlast, dbias1, dbias0

    def fold(product):
        return product[0:64] + product[64:128]

    def finish(net, scale, shift, dm2, ah, af, al, pts, dlast, dbias1, dbias0, extra):
        lane = lax.broadcasted_iota(jnp.int32, (64, 128), 1)
        pts = jnp.where(lane == 4, dbias0, pts)
        pts = jnp.where(lane == 5, dbias1, pts)
        pts = jnp.where(lane == 6, dlast, pts)
        turned = pts.T
        sums = turned[0:8] + turned[8:16]
        m1 = nets[net, 0:64, 0:64]
        rows = nets[net, 64:72, 0:64]
        row = [scale[d] * rows[d : d + 1] for d in range(3)]
        square = row[0] * row[0] + row[1] * row[1] + row[2] * row[2]
        dsquare = -2.0 * jnp.sum(m1 * al, axis=0, keepdims=True)
        dm1 = ah - 2.0 * (al * square)
        first = []
        for d in range(3):
            dm1 = dm1 + af[d] * row[d]
            slope = sums[d : d + 1] + jnp.sum(m1 * af[d], axis=0, keepdims=True) + 2.0 * row[d] * dsquare
            first.append(scale[d] * slope + shift[d] * sums[3:4])
        grads[net, 0:64, :] = jnp.concatenate([dm1, dm2], 1)
        grads[net, 64:72, 0:64] = jnp.concatenate(first + [sums[3:7], extra], 0)
        grads[net, 64:72, 64:128] = jnp.zeros((8, 64), f32)

    def wide_tools(net):
        def get(k):
            return cols[net, :, k : k + 1]

        def mm(ref, low, high, streams):
            out = dot(ref[net, low:high, :], jnp.concatenate(streams, 1))
            return [out[:, count * k : count * (k + 1)] for k in range(len(streams))]

        return get, mm

    def row_sums(value):
        return jnp.sum(value, axis=1, keepdims=True)

    def forward_wide(net):
        get, mm = wide_tools(net)

        def keep_parts(ref, parts):
            for k, part in enumerate(parts):
                ref[net, k, 0:64, :] = part[0]
                ref[net, k, 64:128, :] = part[1]

        def keep0(h, parts):
            h0s[net] = h
            keep_parts(x0, parts)

        def keep1(values, parts):
            for k, value in enumerate(values):
                a1[net, k] = value
            keep_parts(x1, parts)

        def keep2(values):
            for k, value in enumerate(values):
                a2[net, k] = value

        res[0:1, :] = res[0:1, :] + forward(get, xp[...], alpha[net], mm, keep0, keep1, keep2)

    def sides(value, low=0):
        return value[:, low : low + 64] + value[:, low + 64 : low + 128]

    def both(part):
        return jnp.concatenate(part, 0)

    def backward_wide(net, extra):
        get, mm = wide_tools(net)
        g2, g1, g0, dlast, dbias1, dbias0 = backward(
            get,
            alpha[net],
            res[1:2, :],
            mm,
            row_sums,
            h0s[net],
            [a1[net, k] for k in range(6)],
            [a2[net, k] for k in range(7)],
        )
        dm2 = dot_nt(
            jnp.concatenate([both(g) for g in g2], 1),
            jnp.concatenate([x1[net, k] for k in range(5)], 1),
        )
        ah = dot_nt(both(g1[0]), x0[net, 0])
        af = dot_nt(jnp.concatenate([both(g) for g in g1[1:4]], 0), x0[net, 1])
        al = dot_nt(both(g1[4]), x0[net, 2])
        pts = fold(dot_nt(both(g0), xpb[...]))
        af = [sides(fold(af[128 * d : 128 * (d + 1)])) for d in range(3)]
        scale, shift = affine(net)
        dm2, ah, al = [sides(fold(value)) for value in (dm2, ah, al)]
        finish(net, scale, shift, dm2, ah, af, al, pts, dlast, dbias1, dbias0, extra)

    half = lax.broadcasted_iota(jnp.int32, (1, pair), 1) < slots
    first_half = jnp.where(lower, 1.0, 0.0).astype(bf16)
    second_half = jnp.where(lower, 0.0, 1.0).astype(bf16)

    def face_get(k):
        return fcols[k]

    def face_mm(ref, low, high, streams):
        rows = high - low
        number = len(streams)
        mask = (lax.broadcasted_iota(jnp.int32, (1, number * pair), 1) & (pair - 1)) < slots
        pieces = []
        for axis in range(3):
            net = 3 + 2 * axis
            span = slice(axis * pair, (axis + 1) * pair)
            lhs = jnp.concatenate([ref[net, low:high, :], ref[net + 1, low:high, :]], 0)
            out = dot(lhs, jnp.concatenate([stream[:, span] for stream in streams], 1))
            out = jnp.where(mask, out[0:rows], out[rows : 2 * rows])
            pieces.append([out[:, pair * k : pair * (k + 1)] for k in range(number)])
        return [jnp.concatenate([piece[k] for piece in pieces], 1) for k in range(number)]

    def half_sums(value):
        return [
            row_sums(jnp.where(half if face % 2 == 0 else ~half, value[:, pair * (face // 2) : pair * (face // 2 + 1)], 0.0))
            for face in range(6)
        ]

    def forward_faces():
        def keep_parts(ref, parts):
            for k, part in enumerate(parts):
                ref[k, 0:64, :] = part[0] * first_half
                ref[k, 64:128, :] = part[1] * first_half
                ref[k, 128:192, :] = part[0] * second_half
                ref[k, 192:256, :] = part[1] * second_half

        def keep0(h, parts):
            fh0s[...] = h
            keep_parts(fx0, parts)

        def keep1(values, parts):
            for k, value in enumerate(values):
                fa1[k] = value
            keep_parts(fx1, parts)

        def keep2(values):
            for k, value in enumerate(values):
                fa2[k] = value

        row = forward(face_get, xf[...], falpha[...], face_mm, keep0, keep1, keep2)
        terms = jnp.concatenate([term.astype(f32) for term in three(row)] + [jnp.zeros((5, near), f32)], 0)
        spread = dot_nt(terms.astype(bf16), hot[...])
        res[0:1, :] = res[0:1, :] + (spread[0:1] + spread[1:2] + spread[2:3])

    def backward_faces():
        g2, g1, g0, dlast, dbias1, dbias0 = backward(
            face_get,
            falpha[...],
            fdelta[0:1, :],
            face_mm,
            half_sums,
            fh0s[...],
            [fa1[k] for k in range(6)],
            [fa2[k] for k in range(7)],
        )
        for axis in range(3):
            span = slice(axis * pair, (axis + 1) * pair)

            def cut(part):
                return jnp.concatenate([part[0][:, span], part[1][:, span]], 0)

            dm2 = fold(
                dot_nt(
                    jnp.concatenate([cut(g) for g in g2], 1),
                    jnp.concatenate([fx1[k, :, span] for k in range(5)], 1),
                )
            )
            ah = fold(dot_nt(cut(g1[0]), fx0[0, :, span]))
            af = dot_nt(jnp.concatenate([cut(g) for g in g1[1:4]], 0), fx0[1, :, span])
            af = [fold(af[128 * d : 128 * (d + 1)]) for d in range(3)]
            al = fold(dot_nt(cut(g1[4]), fx0[2, :, span]))
            for side in range(2):
                face = 2 * axis + side
                kept = (first_half if side == 0 else second_half)[:, span]
                pts = fold(dot_nt(cut(g0), xfb[:, span] * kept))
                scale, shift = face_affine(face)
                finish(
                    3 + face,
                    scale,
                    shift,
                    sides(dm2, 128 * side),
                    sides(ah, 128 * side),
                    [sides(v, 128 * side) for v in af],
                    sides(al, 128 * side),
                    pts,
                    dlast[face],
                    dbias1[face],
                    dbias0[face],
                    jnp.zeros((1, 64), f32),
                )

    def total(ref, number):
        value = ref[0]
        for k in range(1, number):
            value = value + ref[k]
        return value

    def tile_copy(tile):
        return pltpu.make_async_remote_copy(
            src_ref=grads.at[0, 8 * tile : 8 * tile + 8, :],
            dst_ref=tiles.at[here],
            send_sem=tile_send.at[tile],
            recv_sem=tile_recv.at[here],
            device_id=(owners[tile] // sizes[1], owners[tile] % sizes[1], me[2]),
            device_id_type=MESH,
        )

    def tile_arrival(sender):
        return pltpu.make_async_remote_copy(
            src_ref=grads.at[0, 0:8, :],
            dst_ref=tiles.at[sender],
            send_sem=tile_send.at[0],
            recv_sem=tile_recv.at[sender],
            device_id=in_plane(sender),
            device_id_type=MESH,
        )

    def along_z(source_ref, ref, send, recv, offset, sender):
        return pltpu.make_async_remote_copy(
            src_ref=source_ref,
            dst_ref=ref.at[sender],
            send_sem=send.at[offset],
            recv_sem=recv.at[sender],
            device_id=peer(2, offset),
            device_id_type=MESH,
        )

    def level_copy(offset, arriving):
        sender = lax.rem(me[2] + (sizes[2] - offset), sizes[2]) if arriving else me[2]
        return along_z(levels.at[me[2]], levels, level_send, level_recv, offset, sender)

    layers = -(-TILES // sizes[2])

    def column_copies(offset, arriving):
        target = lax.rem(me[2] + offset, sizes[2])
        sender = lax.rem(me[2] + (sizes[2] - offset), sizes[2]) if arriving else me[2]
        for layer in range(layers):
            tile = layer * sizes[2] + (me[2] if arriving else target)
            rows = pl.ds(pl.multiple_of(8 * lax.rem(tile, TILES), 8), 8)
            yield tile < TILES, pltpu.make_async_remote_copy(
                src_ref=grads.at[1, rows, :],
                dst_ref=columns.at[layer, sender],
                send_sem=column_send.at[layer, offset],
                recv_sem=column_recv.at[layer, sender],
                device_id=peer(2, offset),
                device_id_type=MESH,
            )

    def gather_copies(offset, arriving):
        sender = lax.rem(me[2] + (sizes[2] - offset), sizes[2]) if arriving else me[2]
        for layer in range(layers):
            tile = layer * sizes[2] + sender
            rows = pl.ds(pl.multiple_of(8 * lax.rem(tile, TILES), 8), 8)
            yield tile < TILES, pltpu.make_async_remote_copy(
                src_ref=column_sum.at[rows, :],
                dst_ref=column_sum.at[rows, :],
                send_sem=gather_send.at[layer, offset],
                recv_sem=gather_recv.at[layer, sender],
                device_id=peer(2, offset),
                device_id_type=MESH,
            )

    def own_layers():
        for layer in range(layers):
            tile = layer * sizes[2] + me[2]
            yield layer, tile < TILES, pl.ds(pl.multiple_of(8 * lax.rem(tile, TILES), 8), 8)

    def every(copies, arriving, action):
        for offset in range(1, sizes[2]):
            for needed, copy in copies(offset, arriving):
                pl.when(needed)(getattr(copy, action))

    def share_copy(number):
        x, y = far_first(sizes)[number]
        target = (lax.rem(me[0] + x, sizes[0]), lax.rem(me[1] + y, sizes[1]), me[2])
        return pltpu.make_async_remote_copy(
            src_ref=summed.at[my_rows, :],
            dst_ref=summed.at[my_rows, :],
            send_sem=share_send.at[number],
            recv_sem=share_recv.at[my_tile],
            device_id=target,
            device_id_type=MESH,
        )

    def share_arrival(tile):
        rows = summed.at[8 * tile : 8 * tile + 8, :]
        return pltpu.make_async_remote_copy(
            src_ref=rows,
            dst_ref=rows,
            send_sem=share_send.at[0],
            recv_sem=share_recv.at[tile],
            device_id=in_plane(owners[tile]),
            device_id_type=MESH,
        )

    def send_back(face):
        axis, up = face // 2, face % 2
        return pltpu.make_async_remote_copy(
            src_ref=grads.at[3 + face],
            dst_ref=back.at[face ^ 1],
            send_sem=back_send.at[face],
            recv_sem=back_recv.at[face ^ 1],
            device_id=peer(axis, 2 * up - 1),
            device_id_type=MESH,
        )

    def give(value, first_ref, mid_ref, last_ref):
        mid_ref[0] = value[0:64, 0:64]
        mid_ref[1] = value[0:64, 64:128]
        first_ref[...] = value[64:68, 0:64]
        for k in range(3):
            if len(last_ref.shape) == 3:
                last_ref[k] = value[68 + k : 69 + k, 0:64]
            else:
                last_ref[k : k + 1, :] = value[68 + k : 69 + k, 0:64]

    res[0:1, :] = -source[...]

    for net in range(3):
        prepare_forward(net, *affine(net))
        forward_wide(net)
        if net == 0:
            hear(1)
            greet(2)
    hear(2)
    greet(3)
    prepare_backward(0)
    for face in faces:
        halo(face).wait_recv()
    for face in range(6):
        prepare_forward(3 + face, *face_affine(face))
    for k in range(7):
        fcols[k] = jnp.concatenate(
            [
                jnp.where(half, cols[3 + 2 * axis, :, k : k + 1], cols[4 + 2 * axis, :, k : k + 1])
                for axis in range(3)
            ],
            1,
        )
    forward_faces()

    residual = res[0:1, :]
    residual_out[...] = residual
    delta = residual * (1.0 / count)
    res[1:2, :] = delta
    loss = jnp.sum(residual * residual, axis=1, keepdims=True) * (0.5 / count)

    first_lane = lax.broadcasted_iota(jnp.int32, (1, 64), 1) == 0
    backward_wide(0, jnp.where(first_lane, loss, 0.0))
    hear(3)
    for tile in range(TILES):
        pl.when(here != owners[tile])(tile_copy(tile).start)

    prepare_backward(1)
    backward_wide(1, jnp.zeros((1, 64), f32))
    every(column_copies, False, "start")

    terms = jnp.concatenate([term.astype(f32) for term in three(delta)] + [jnp.zeros((5, count), f32)], 0)
    taken = dot(terms.astype(bf16), hot[...])
    fdelta[0:1, :] = taken[0:1] + taken[1:2] + taken[2:3]

    for face in range(6):
        prepare_backward(3 + face)
    backward_faces()
    for face in faces:
        send_back(face).start()

    @pl.when(reducer)
    def _():
        tiles[here] = grads[0, my_rows, :]
        for offset in range(1, plane):
            tile_arrival(lax.rem(here + offset, plane)).wait_recv()
        levels[me[2]] = total(tiles, plane)
        for offset in range(1, sizes[2]):
            level_copy(offset, False).start()

    prepare_backward(2)
    backward_wide(2, jnp.zeros((1, 64), f32))

    for layer, needed, rows in own_layers():

        @pl.when(needed)
        def _(layer=layer, rows=rows):
            columns[layer, me[2]] = grads[1, rows, :]

    every(column_copies, True, "wait_recv")
    for layer, needed, rows in own_layers():

        @pl.when(needed)
        def _(layer=layer, rows=rows):
            column_sum[rows, :] = total(columns.at[layer], sizes[2])

    every(gather_copies, False, "start")

    for face in faces:
        send_back(face).wait()
    give(grads[2] + total(back, 6), fine_first_out, fine_mid_out, fine_last_out)

    @pl.when(reducer)
    def _():
        for offset in range(1, sizes[2]):
            level_copy(offset, True).wait_recv()
        summed[my_rows, :] = total(levels, sizes[2])
        for number in range(plane - 1):
            share_copy(number).start()

    every(gather_copies, True, "wait_recv")
    give(column_sum[...], column_first_out, column_mid_out, column_last_out)
    every(column_copies, False, "wait_send")
    every(gather_copies, False, "wait_send")
    for tile in range(TILES):
        pl.when(here != owners[tile])(tile_copy(tile).wait_send)
    for face in faces:
        halo(face).wait_send()

    @pl.when(reducer)
    def _():
        for offset in range(1, sizes[2]):
            level_copy(offset, False).wait_send()
        for number in range(plane - 1):
            share_copy(number).wait_send()

    for tile in range(TILES):
        rows = slice(8 * tile, 8 * tile + 8)
        pl.when(here != owners[tile])(share_arrival(tile).wait_recv)
        if tile < TILES - 1:
            global_mid_out[0, rows, :] = summed[rows, 0:64]
            global_mid_out[1, rows, :] = summed[rows, 64:128]
    value = summed[64:72, :]
    global_first_out[...] = value[0:4, 0:64]
    global_last_out[...] = value[4:7, 0:64]
    loss_out[...] = value[7:8, 0:1]


def hand_over(*refs):
    number = len(refs) // 2
    ins, outs, sem = refs[:number], refs[number : 2 * number], refs[2 * number]
    copies = [pltpu.make_async_copy(ins[k], outs[k], sem.at[k]) for k in range(number)]
    for copy in copies:
        copy.start()
    for copy in copies:
        copy.wait()


def step(sizes, points, band_index, source, *params):
    count = points.shape[-1]
    slots = band_index.shape[-1]
    near = 6 * slots
    plane = sizes[0] * sizes[1]
    layers = -(-TILES // sizes[2])
    operands = [points.reshape(3, 1, count), band_index.reshape(6, 1, slots), source.reshape(1, count)]
    shapes = [(4, 64), (2, 64, 64), (3, 1, 64)] * 2 + [(4, 64), (2, 64, 64), (3, 64)]
    operands += [param.reshape(shape) for param, shape in zip(params, shapes)]
    outs = [jax.ShapeDtypeStruct(shape, f32) for shape in [(1, count)] + shapes + [(1, 1)]]
    vmem = pltpu.VMEM
    scratch = [vmem(value.shape, value.dtype) for value in operands]
    scratch += [
        vmem((9, 72, 128), f32),
        vmem((9, 72, 128), f32),
        vmem((9, 320, 192), bf16),
        vmem((9, 64, 192), bf16),
        vmem((9, 64, 192), bf16),
        vmem((9, 64, 192), bf16),
        vmem((9, 64, 576), bf16),
        vmem((9, 64, 192), bf16),
        vmem((9, 64, 128), f32),
        vmem((8, count), f32),
        vmem((128, count), bf16),
        vmem((3, 8, count), f32),
        vmem((3, 3, 128, count), bf16),
        vmem((3, 5, 128, count), bf16),
        vmem((3, 64, count), f32),
        vmem((3, 6, 64, count), f32),
        vmem((3, 7, 64, count), f32),
        vmem((8, count), f32),
        vmem((8, near), f32),
        vmem((128, near), bf16),
        vmem((8, near), f32),
        vmem((7, 64, near), f32),
        vmem((3, 256, near), bf16),
        vmem((5, 256, near), bf16),
        vmem((64, near), f32),
        vmem((6, 64, near), f32),
        vmem((7, 64, near), f32),
        vmem((8, near), f32),
        vmem((count, near), bf16),
        vmem((6, 72, 128), f32),
        vmem((plane, 8, 128), f32),
        vmem((sizes[2], 8, 128), f32),
        vmem((72, 128), f32),
        vmem((layers, sizes[2], 8, 128), f32),
        vmem((72, 128), f32),
    ]
    dma = pltpu.SemaphoreType.DMA
    scratch += [dma((12,))] + [dma((6,))] * 4
    scratch += [dma((number,)) for number in (TILES, plane, sizes[2], sizes[2], plane, TILES)]
    scratch += [dma((layers, sizes[2]))] * 4 + [pltpu.SemaphoreType.REGULAR((3,))]
    whole = pl.BlockSpec(memory_space=pltpu.VMEM)
    outside = pl.BlockSpec(memory_space=pltpu.HBM)
    results = pl.pallas_call(
        functools.partial(kernel, sizes),
        out_shape=[vmem(value.shape, value.dtype) for value in outs],
        in_specs=[outside] * 12,
        out_specs=[whole] * 11,
        scratch_shapes=scratch,
        compiler_params=pltpu.CompilerParams(
            collective_id=0, has_side_effects=True, vmem_limit_bytes=32 << 20
        ),
        cost_estimate=pl.CostEstimate(flops=500_000_000, bytes_accessed=1_000_000, transcendentals=400_000),
        name="training_step",
    )(*[pltpu.with_memory_space_constraint(value, pltpu.HBM) for value in operands])
    results = pl.pallas_call(
        hand_over,
        out_shape=outs,
        in_specs=[whole] * 11,
        out_specs=[outside] * 11,
        scratch_shapes=[dma((11,))],
        compiler_params=pltpu.CompilerParams(vmem_limit_bytes=1 << 20),
        cost_estimate=pl.CostEstimate(flops=0, bytes_accessed=400_000, transcendentals=0),
        name="hand_over",
    )(*results)
    ranks = [params[k].shape for k in range(9)]
    arrays = [results[0].reshape(source.shape)]
    arrays += [value.reshape(shape) for value, shape in zip(results[1:10], ranks)]
    return tuple(arrays) + (results[10].reshape(()),)


def solution(mesh):
    sizes = tuple(mesh.shape[axis] for axis in AXES)
    cell = ("gx", "gy", "gz")
    column = ("gx", "gy")
    in_specs = (P(*cell, None, None), P(*cell, None, None), P(*cell, None))
    nets_specs = (
        (P(*cell, None, None), P(*cell, None, None, None), P(*cell, None, None))
        + (P(*column, None, None), P(*column, None, None, None), P(*column, None, None))
        + (P(), P(), P())
    )
    return jax.shard_map(
        functools.partial(step, sizes),
        mesh=mesh,
        in_specs=in_specs + nets_specs,
        out_specs=(P(*cell, None),) + nets_specs + (P(),),
        check_vma=False,
    )
```
